256 devices in a mesh: group: 4 (over y), dev: 64 (over x, z, core).
Axes of the slice: x: 4, y: 4, z: 8, core: 2. Of those that a mesh axis runs over, the one named last changes fastest.
Arguments:
- embeddings: bfloat16 [131072, 768], P(('group', 'dev')), may hold values from -6 to 6
- cluster: int32 [131072], P(('group', 'dev')), may hold values from 0 to 31, as said below
- order: int32 [131072], P(('group', 'dev')), may hold values from 0 to 131071, as said below
- query_local: int32 [16384], P(('group', 'dev')), may hold values from 0 to 511, as said below
Outputs:
- best: float32 [16384], P(('group', 'dev'))
The draws below stay inside these ranges and needn't reach their ends.
Inputs may be any that keep to these rules, and one draw needn't show every extreme that they name: Each value is a cluster of 0 to 31; among the rows of one data owner (aligned blocks of 512 rows), at most 256 lie in clusters with one value of cluster modulo 4, and in every block some residue has exactly 256. `order`: all values are distinct: a permutation of 0 to 131071. `query_local`: each aligned block of 64 entries holds distinct row indices of one data owner; its i-th run of 16 entries names rows whose cluster modulo 4 equals i.
All inputs are finite; a program needn't handle non-finite values.
Results may differ from the reference program's by a relative error of at most 0.0013.
Values may be sent and summed in bfloat16 or wider, within the bound.
A program may use at most 128 MiB of HBM per device.

```python
import jax
import jax.numpy as jnp
from jax import lax

D = 768
ROWS_DEV = 512
QCAP = 16
QRY_DEV = 64
ROWS = 131072
NQ = 16384


def layout(key):
    blocks = ROWS // ROWS_DEV
    first, second = jax.random.split(jax.random.fold_in(key, 11), 2)
    ranks = jnp.arange(ROWS_DEV, dtype=jnp.int32)
    rank_group = (ranks >= ROWS_DEV // 2).astype(jnp.int32) + (ranks >= 3 * ROWS_DEV // 4).astype(jnp.int32) + (ranks >= 7 * ROWS_DEV // 8).astype(jnp.int32)
    rotation = jax.random.randint(first, (blocks,), 0, 4).astype(jnp.int32)
    placing = jax.vmap(lambda item: jax.random.permutation(item, ROWS_DEV))(jax.random.split(second, blocks)).astype(jnp.int32)
    return (rank_group, rotation, placing)


def draw_cluster(key, part):
    rank_group, rotation, placing = layout(key)
    key = jax.random.fold_in(key, 1)
    blocks = ROWS // ROWS_DEV
    key_a, key_b, key_c = jax.random.split(key, 3)
    home = (rank_group[None, :] + rotation[:, None]) % 4
    first_pick = jax.random.randint(key_a, (blocks, ROWS_DEV), 0, 8)
    second_pick = jax.random.randint(key_b, (blocks, ROWS_DEV), 0, 8)
    member = first_pick * (second_pick + 1) // 8
    table = jax.vmap(lambda item: jax.random.permutation(item, 8))(jax.random.split(key_c, 4)).astype(jnp.int32)
    ranked = home + 4 * table[home, member]
    rows_index = jnp.arange(blocks)[:, None]
    placed = jnp.zeros((blocks, ROWS_DEV), jnp.int32).at[rows_index, placing].set(ranked.astype(jnp.int32))
    return placed.reshape(ROWS)


def draw_order(key, part):
    key = jax.random.fold_in(key, 3)
    return jax.random.permutation(key, ROWS).astype(jnp.int32)


def draw_query_local(key, part):
    rank_group, rotation, placing = layout(key)
    key = jax.random.fold_in(key, 2)
    blocks = ROWS // ROWS_DEV
    starts = jnp.array([0, ROWS_DEV // 2, 3 * ROWS_DEV // 4, 7 * ROWS_DEV // 8], jnp.int32)
    homes = jnp.arange(4, dtype=jnp.int32)
    which = (homes[None, :] - rotation[:, None]) % 4
    picks = jax.vmap(lambda item: jax.random.permutation(item, ROWS_DEV // 8)[:QCAP])(jax.random.split(key, blocks * 4)).astype(jnp.int32)
    picks = picks.reshape(blocks, 4, QCAP)
    ranks = starts[which][:, :, None] + picks
    rows_index = jnp.arange(blocks)[:, None, None]
    chosen = placing[rows_index, ranks]
    return chosen.reshape(NQ).astype(jnp.int32)


def levels(key, shape, shards, smallest, largest):
    def one(axis_at, blocks):
        heights = jax.random.uniform(jax.random.fold_in(jax.random.fold_in(key, 6), axis_at), (blocks,), jnp.float32, smallest / len(shards), largest / len(shards))
        return jnp.repeat(jnp.exp(heights), shape[axis_at] // blocks).reshape((-1,) + (1,) * (len(shape) - axis_at - 1))

    gain = one(*shards[0])
    for cut in shards[1:]:
        gain = gain * one(*cut)
    return gain


def scatter_about(rng, shape, spread, bound, cuts=(), held_as=jnp.bfloat16):
    result = spread * jax.random.normal(rng, shape, jnp.float32)
    if cuts:
        result = result * levels(rng, shape, cuts, -0.22, 0.18)
    return jnp.clip(result, -bound, bound).astype(held_as)


def setup_inputs(seed: int = 0) -> dict:
    key_of = jax.random.split(jax.random.key(seed), 5)
    embeddings = scatter_about(key_of[0], (ROWS, D), 1.0, 6.0, ((0, 256),))
    cluster = draw_cluster(jax.random.fold_in(key_of[4], 71), 0)
    order = draw_order(jax.random.fold_in(key_of[4], 71), 0)
    query_local = draw_query_local(jax.random.fold_in(key_of[4], 71), 0)
    return dict(embeddings=embeddings, cluster=cluster, order=order, query_local=query_local)


def normalize(rows):
    wide = rows.astype(jnp.float32)
    total = lax.optimization_barrier(jnp.sum(wide * wide, axis=-1))
    return (wide * lax.rsqrt(total + 1e-06)[:, None]).astype(jnp.bfloat16)

def reference(embeddings, cluster, order, query_local):
    unit = normalize(embeddings)
    owner = jnp.arange(NQ, dtype=jnp.int32) // QRY_DEV
    global_row = owner * ROWS_DEV + query_local
    queries = unit[global_row]
    query_clu = cluster[global_row]
    query_ord = order[global_row]
    block = ROWS_DEV * 8
    keys = unit.reshape(ROWS // block, block, D)
    key_clu = cluster.reshape(ROWS // block, block)
    key_ord = order.reshape(ROWS // block, block)

    def step(carry, items):
        key_rows, clu_rows, ord_rows = items
        scores = jnp.dot(queries, key_rows.T, preferred_element_type=jnp.float32)
        keep = (query_clu[:, None] == clu_rows[None, :]) & (ord_rows[None, :] < query_ord[:, None])
        local = lax.optimization_barrier(jnp.max(jnp.where(keep, scores, jnp.float32(-1.0)), axis=1))
        return (jnp.maximum(carry, local), None)
    start = jnp.full((NQ,), -1.0, jnp.float32)
    best, unused = lax.scan(step, start, (keys, key_clu, key_ord))
    return best
```

```python
import jax
import jax.numpy as jnp
from jax import lax
from jax.experimental import pallas as pl
from jax.experimental.pallas import tpu as pltpu
from jax.sharding import PartitionSpec as P

MESH = pl.DeviceIdType.MESH
F32, BF16 = jnp.float32, jnp.bfloat16
NY, NX, NZ = 4, 4, 8
D = 768
ROWS = 512
QB = 64
RUN = 16
CAP = 256
SPAN = 131072.0


def iota(shape, axis):
    return lax.broadcasted_iota(jnp.int32, shape, axis)


def meta_tile(picked):
    order = picked[1:2] + 256.0 * picked[2:3] + 65536.0 * picked[3:4]
    return jnp.where(iota(picked.shape, 0) == 0, picked[0:1], order)


def kernel(
    emb_ref, clu_ref, ord_ref, qry_ref, out_ref,
    unit, qsel, qmsrc, qmrecv, ksel, kmsrc, kbuf, kmeta, kcode, qbuf, qmeta,
    best, zred, rtile, fin,
    s_qy, s_my, r_qy, r_my, s_k, s_km, r_k, r_km, s_kf, s_kmf,
    s_g, s_gm, r_g, r_gm, s_z, r_z, s_f, r_f,
):
    y = lax.axis_index("group")
    d = lax.axis_index("dev")
    x, z, c = d // (2 * NZ), (d // 2) % NZ, d % 2

    def peer(dy=0, dx=0, dz=0, dc=0):
        return (
            (y + dy) % NY,
            (((x + dx) % NX) * NZ + (z + dz) % NZ) * 2 + (c + dc) % 2,
        )

    def rcopy(src, dst, ssem, rsem, to):
        return pltpu.make_async_remote_copy(
            src_ref=src, dst_ref=dst, send_sem=ssem, recv_sem=rsem,
            device_id=to, device_id_type=MESH,
        )

    barrier = pltpu.get_barrier_semaphore()
    greeted = [peer(dz=k) for k in range(1, NZ)] + [peer(dc=1)]
    greeted += [peer(dy=k // NX, dx=k % NX) for k in range(1, NY * NX)]
    for to in greeted:
        pl.semaphore_signal(barrier, inc=1, device_id=to, device_id_type=MESH)

    wide = emb_ref[...].astype(F32)
    total = jnp.sum(wide * wide, axis=-1, keepdims=True)
    unit[...] = (wide * lax.rsqrt(total + 1e-06)).astype(BF16)

    clu, order = clu_ref[...], ord_ref[...]
    row = iota((8, ROWS), 0)
    digits = jnp.where(
        row == 0,
        clu + 1,
        jnp.where(
            row == 1,
            order & 255,
            jnp.where(row == 2, (order >> 8) & 255, jnp.where(row == 3, order >> 16, 0)),
        ),
    ).astype(F32).astype(BF16)

    lanes = jnp.concatenate([qry_ref[...], qry_ref[...]], axis=1).astype(F32)
    column = jnp.transpose(jnp.broadcast_to(lanes, (128, 128)))[:QB]
    column = jnp.concatenate([column] * (ROWS // 128), axis=1)
    pick = jnp.where(column == iota((QB, ROWS), 1).astype(F32), 1.0, 0.0).astype(BF16)
    qsel[...] = jnp.dot(pick, unit[...], preferred_element_type=F32).astype(BF16)
    picked = lax.dot_general(digits, pick, (((1,), (1,)), ((), ())), preferred_element_type=F32)
    picked = meta_tile(jnp.concatenate([picked, picked], axis=1))
    lane = iota((8, 128), 1)
    for i in range(NY):
        tile = jnp.where((lane // RUN) % NY == i, picked, 0.0)
        tile = tile + pltpu.roll(tile, RUN, 1)
        qmsrc[i] = tile + pltpu.roll(tile, 2 * RUN, 1)

    pl.semaphore_wait(barrier, len(greeted))

    def run_at(which):
        return pl.ds(pl.multiple_of(which * RUN, RUN), RUN)

    def block_at(which):
        return pl.ds(pl.multiple_of(which * QB, QB), QB)

    here = pl.ds(pl.multiple_of(x * QB + y * RUN, RUN), RUN)
    for k in range(1, NY):
        i = (y + k) % NY
        rcopy(qsel.at[run_at(i)], qbuf.at[z, here], s_qy.at[k], r_qy.at[y], peer(dy=k)).start()
        rcopy(qmsrc.at[i], qmrecv.at[y], s_my.at[k], r_my.at[y], peer(dy=k)).start()
    qbuf[z, here] = qsel[run_at(y)]
    qmrecv[y] = qmsrc[y]

    residue = clu % NY
    member = jnp.where(row == residue, 1.0, 0.0)
    before = jnp.where(iota((ROWS, ROWS), 0) < iota((ROWS, ROWS), 1), 1.0, 0.0).astype(BF16)
    prefix = jnp.dot(member.astype(BF16), before, preferred_element_type=F32)
    rank = jnp.sum(member * prefix, axis=0, keepdims=True)
    dest = residue.astype(F32) * CAP + rank
    slot = iota((CAP, ROWS), 0)

    def of_residue(r):
        place = jnp.where((slot + r * CAP).astype(F32) == dest, 1.0, 0.0).astype(BF16)
        rows = jnp.dot(place, unit[...], preferred_element_type=F32).astype(BF16)
        tile = lax.dot_general(digits, place, (((1,), (1,)), ((), ())), preferred_element_type=F32)
        return rows, meta_tile(tile)

    def half(which):
        return pl.ds(pl.multiple_of(which * CAP, CAP), CAP)

    def key_send(k):
        to = peer(dy=k)
        rcopy(ksel.at[k], kbuf.at[y, half(c)], s_k.at[k], r_k.at[y, c], to).start()
        rcopy(kmsrc.at[k], kmeta.at[y, c], s_km.at[k], r_km.at[y, c], to).start()

    def key_select(k):
        rows, tile = of_residue((y + k) % NY)
        ksel[k] = rows
        kmsrc[k] = tile

    def key_wait(ys, cs):
        rcopy(kbuf.at[ys, half(cs)], kbuf.at[ys, half(cs)], s_kf.at[0], r_k.at[ys, cs], peer(dc=1)).wait_recv()
        rcopy(kmeta.at[ys, cs], kmeta.at[ys, cs], s_kmf.at[0], r_km.at[ys, cs], peer(dc=1)).wait_recv()

    def key_share(k):
        ys = (y + k) % NY
        at = kbuf.at[ys, half(c)]
        rcopy(at, at, s_kf.at[k], r_k.at[ys, c], peer(dc=1)).start()
        rcopy(kmeta.at[ys, c], kmeta.at[ys, c], s_kmf.at[k], r_km.at[ys, c], peer(dc=1)).start()

    def key_codes(k):
        ys = (y + k) % NY
        for cs in range(2):
            tile = kmeta[ys, cs]
            code = (tile[0:1] - 1.0) * SPAN + tile[1:2]
            kcode[ys, cs * CAP:(cs + 1) * CAP, :] = jnp.transpose(jnp.broadcast_to(code, (128, CAP)))

    for k in (1, 3, 2):
        key_select(k)
        key_send(k)
    rows, tile = of_residue(y)
    kbuf[y, half(c)] = rows
    kmeta[y, c] = tile
    key_share(0)

    for k in range(1, NY):
        ys = (y + k) % NY
        at = pl.ds(pl.multiple_of(x * QB + ys * RUN, RUN), RUN)
        rcopy(qsel.at[run_at(ys)], qbuf.at[z, at], s_qy.at[k], r_qy.at[ys], peer(dy=k)).wait_recv()
        rcopy(qmsrc.at[ys], qmrecv.at[ys], s_my.at[k], r_my.at[ys], peer(dy=k)).wait_recv()
    own = qmrecv[0]
    for i in range(1, NY):
        own = jnp.where((lane // RUN) % NY == i, qmrecv[i], own)
    qmeta[z, x] = own

    def block(dx, dz):
        return (x + dx) % NX, (z + dz) % NZ

    def send(count, at, to):
        xs, zs = at
        n = count[0]
        count[0] += 1
        rows = qbuf.at[zs, block_at(xs)]
        rcopy(rows, rows, s_g.at[n], r_g.at[zs, xs], to).start()
        tile = qmeta.at[zs, xs]
        rcopy(tile, tile, s_gm.at[n], r_gm.at[zs, xs], to).start()

    def arrive(at):
        xs, zs = at
        rows = qbuf.at[zs, block_at(xs)]
        rcopy(rows, rows, s_g.at[0], r_g.at[zs, xs], peer(dc=1)).wait_recv()
        tile = qmeta.at[zs, xs]
        rcopy(tile, tile, s_gm.at[0], r_gm.at[zs, xs], peer(dc=1)).wait_recv()

    def along_x(count, at):
        for dx in (1, 3, 2):
            send(count, at, peer(dx=dx))

    sent = ([0], [0])

    def x_start():
        count = sent[0]
        along_x(count, block(0, 0))
        send(count, block(0, 0), peer(dz=1))
        send(count, block(0, 0), peer(dz=-1))
        for dx in (1, 3, 2):
            arrive(block(dx, 0))
            send(count, block(dx, 0), peer(dz=1))
            send(count, block(dx, 0), peer(dz=-1))

    def turn(dx):
        return 1 - 2 * (((x + dx) % NX) % 2)

    def x_step(s):
        count = sent[0]
        for dx in range(NX):
            if s == 4:
                arrive(block(dx, 4))
                continue
            arrive(block(dx, -s))
            if s < 3:
                send(count, block(dx, -s), peer(dz=1))
            arrive(block(dx, s))
            if s < 3:
                send(count, block(dx, s), peer(dz=-1))
            else:
                send(count, block(dx, -3 * turn(dx)), peer(dz=turn(dx)))

    def z_start():
        count = sent[1]
        send(count, block(0, 0), peer(dz=1))
        send(count, block(0, 0), peer(dz=-1))
        along_x(count, block(0, 0))
        x_wait(0)

    def z_step(s):
        count = sent[1]
        if s == 4:
            arrive(block(0, 4))
            along_x(count, block(0, 4))
            return
        arrive(block(0, -s))
        if s < 3:
            send(count, block(0, -s), peer(dz=1))
        along_x(count, block(0, -s))
        arrive(block(0, s))
        if s < 3:
            send(count, block(0, s), peer(dz=-1))
        else:
            send(count, block(0, -3 * turn(0)), peer(dz=turn(0)))
        along_x(count, block(0, s))

    def x_wait(s):
        for dz in ((s,) if s in (0, 4) else (-s, s)):
            for dx in (1, 3, 2):
                arrive(block(dx, dz))

    def by_core(first, second):
        pl.when(c == 0)(first)
        pl.when(c == 1)(second)

    def slab(i):
        return (z + NZ + (1 - 2 * (i % 2)) * ((i + 1) // 2)) % NZ

    def score(i, j):
        zs = slab(i)
        ys = (y + j + (j // 2) * (5 - 2 * j)) % NY
        s = lax.dot_general(kbuf[ys], qbuf[zs], (((1,), (1,)), ((), ())), preferred_element_type=F32)
        code = kcode[ys]
        for p in range(2):
            tile = jnp.where(lane < QB, qmeta[zs, 2 * p], qmeta[zs, 2 * p + 1])
            low = (tile[0:1] - 1.0) * SPAN
            high = low + tile[1:2]
            keep = (code >= low) & (code < high)
            top = jnp.max(jnp.where(keep, s[:, p * 128:(p + 1) * 128], -1.0), axis=0, keepdims=True)
            best[zs, p:p + 1, :] = jnp.maximum(best[zs, p:p + 1, :], top)

    def rect(i0, i1, j0, j1):
        nj = j1 - j0

        def one(t, carry):
            score(i0 + t // nj, j0 + t % nj)
            return carry

        lax.fori_loop(0, (i1 - i0) * nj, one, 0)

    def slab_copy(i):
        zs = slab(i)
        return rcopy(best.at[zs], zred.at[z], s_z.at[i], r_z.at[z], (y, (x * NZ + zs) * 2 + c))

    best[...] = jnp.full(best.shape, -1.0, F32)

    by_core(x_start, z_start)
    key_wait(y, 1 - c)
    key_codes(0)
    rect(0, 1, 0, 1)

    def z_two():
        z_step(1)
        z_step(2)
        x_wait(1)

    by_core(lambda: x_step(1), z_two)
    rect(1, 3, 0, 1)
    for k in (1, 3):
        key_wait((y + k) % NY, c)
        key_share(k)
    for k in (1, 3):
        key_wait((y + k) % NY, 1 - c)
        key_codes(k)
    rect(0, 3, 1, 3)

    def z_three():
        z_step(3)
        x_wait(2)

    by_core(lambda: x_step(2), z_three)
    rect(3, 5, 0, 3)

    def z_four():
        z_step(4)
        x_wait(3)

    by_core(lambda: x_step(3), z_four)
    rect(5, 7, 0, 3)
    key_wait((y + 2) % NY, c)
    key_share(2)
    key_wait((y + 2) % NY, 1 - c)
    key_codes(2)
    rect(0, 7, 3, 4)
    for i in range(1, 7):
        slab_copy(i).start()
    by_core(lambda: x_step(4), lambda: x_wait(4))
    rect(7, 8, 0, 4)
    slab_copy(7).start()

    top = best[z]
    for k in range(1, NZ):
        zs = (z + k) % NZ
        rcopy(best.at[zs], zred.at[zs], s_z.at[0], r_z.at[zs], peer(dz=k)).wait_recv()
        top = jnp.maximum(top, zred[zs])
    rtile[...] = top
    for k in range(1, NY * NX):
        to = peer(dy=k // NX, dx=k % NX)
        rcopy(rtile, fin.at[y, x], s_f.at[k], r_f.at[y, x], to).start()
    fin[y, x] = top
    for k in range(1, NY * NX):
        ys, xs = (y + k // NX) % NY, (x + k % NX) % NX
        rcopy(rtile, fin.at[ys, xs], s_f.at[0], r_f.at[ys, xs], peer(dy=k // NX, dx=k % NX)).wait_recv()
    result = jnp.zeros((8, 128), F32)
    for r in range(NY):
        tile = jnp.maximum(jnp.maximum(fin[r, 0], fin[r, 1]), jnp.maximum(fin[r, 2], fin[r, 3]))
        tile = jnp.where(x // 2 == 0, tile[0:1], tile[1:2])
        tile = jnp.broadcast_to(tile, (8, 128))
        tile = pltpu.roll(tile, (r * RUN - (x % 2) * QB - y * RUN + 256) % 128, 1)
        result = jnp.where(lane // RUN == r, tile, result)
    out_ref[...] = result[0:1, 0:QB]

    for k in range(1, NY):
        to = peer(dy=k)
        rcopy(qsel.at[pl.ds(0, RUN)], qbuf.at[z, here], s_qy.at[k], r_qy.at[y], to).wait_send()
        rcopy(qmsrc.at[0], qmrecv.at[0], s_my.at[k], r_my.at[y], to).wait_send()
        rcopy(ksel.at[k], kbuf.at[y, half(c)], s_k.at[k], r_k.at[y, c], to).wait_send()
        rcopy(kmsrc.at[k], kmeta.at[y, c], s_km.at[k], r_km.at[y, c], to).wait_send()
    for k in range(NY):
        at = kbuf.at[y, half(c)]
        rcopy(at, at, s_kf.at[k], r_k.at[y, c], peer(dc=1)).wait_send()
        rcopy(kmeta.at[y, c], kmeta.at[y, c], s_kmf.at[k], r_km.at[y, c], peer(dc=1)).wait_send()
    for n in range(31):
        rows = qbuf.at[z, block_at(x)]
        rcopy(rows, rows, s_g.at[n], r_g.at[z, x], peer(dc=1)).wait_send()
        tile = qmeta.at[z, x]
        rcopy(tile, tile, s_gm.at[n], r_gm.at[z, x], peer(dc=1)).wait_send()
    for i in range(1, NZ):
        slab_copy(i).wait_send()
    for k in range(1, NY * NX):
        rcopy(rtile, fin.at[y, x], s_f.at[k], r_f.at[y, x], peer(dy=k // NX, dx=k % NX)).wait_send()


def body(embeddings, cluster, order, query_local):
    dma = pltpu.SemaphoreType.DMA
    out = pl.pallas_call(
        kernel,
        out_shape=jax.ShapeDtypeStruct((1, QB), F32),
        in_specs=[pl.BlockSpec(memory_space=pltpu.VMEM)] * 4,
        out_specs=pl.BlockSpec(memory_space=pltpu.VMEM),
        scratch_shapes=[
            pltpu.VMEM((ROWS, D), BF16),
            pltpu.VMEM((QB, D), BF16),
            pltpu.VMEM((NY, 8, 128), F32),
            pltpu.VMEM((NY, 8, 128), F32),
            pltpu.VMEM((NY, CAP, D), BF16),
            pltpu.VMEM((NY, 8, CAP), F32),
            pltpu.VMEM((NY, 2 * CAP, D), BF16),
            pltpu.VMEM((NY, 2, 8, CAP), F32),
            pltpu.VMEM((NY, 2 * CAP, 128), F32),
            pltpu.VMEM((NZ, NX * QB, D), BF16),
            pltpu.VMEM((NZ, NX, 8, 128), F32),
            pltpu.VMEM((NZ, 8, 128), F32),
            pltpu.VMEM((NZ, 8, 128), F32),
            pltpu.VMEM((8, 128), F32),
            pltpu.VMEM((NY, NX, 8, 128), F32),
            dma((NY,)), dma((NY,)), dma((NY,)), dma((NY,)),
            dma((NY,)), dma((NY,)), dma((NY, 2)), dma((NY, 2)), dma((NY,)), dma((NY,)),
            dma((31,)), dma((31,)), dma((NZ, NX)), dma((NZ, NX)),
            dma((NZ,)), dma((NZ,)), dma((NY * NX,)), dma((NY, NX)),
        ],
        compiler_params=pltpu.CompilerParams(
            collective_id=0, has_side_effects=True, vmem_limit_bytes=48 * 1024 * 1024
        ),
        name="dedup",
    )(
        embeddings,
        cluster.reshape(1, ROWS),
        order.reshape(1, ROWS),
        query_local.reshape(1, QB),
    )
    return out.reshape(QB)


def solution(mesh):
    return jax.shard_map(
        body,
        mesh=mesh,
        in_specs=(
            P(("group", "dev"), None),
            P(("group", "dev")),
            P(("group", "dev")),
            P(("group", "dev")),
        ),
        out_specs=P(("group", "dev")),
        check_vma=False,
    )
```

```python
import jax
import jax.numpy as jnp
from jax import lax
from jax.experimental import pallas as pl
from jax.experimental.pallas import tpu as pltpu
from jax.sharding import PartitionSpec as P

MESH = pl.DeviceIdType.MESH
F32, BF16 = jnp.float32, jnp.bfloat16
NY, NX, NZ = 4, 4, 8
D = 768
ROWS = 512
QB = 64
RUN = 16
CAP = 256
SPAN = 131072.0


def iota(shape, axis):
    return lax.broadcasted_iota(jnp.int32, shape, axis)


def meta_tile(picked):
    order = picked[1:2] + 256.0 * picked[2:3] + 65536.0 * picked[3:4]
    return jnp.where(iota(picked.shape, 0) == 0, picked[0:1], order)


def kernel(
    emb_hbm, clu_hbm, ord_hbm, qry_hbm, out_ref,
    emb_ref, clu_ref, ord_ref, qry_ref,
    unit, qsel, qmsrc, qmrecv, ksel, kmsrc, kbuf, kmeta, kcode, qbuf, qmeta,
    best, zred, rtile, fin,
    s_in, s_q, s_m, r_q, r_m, s_k, s_km, r_k, r_km, s_kf, s_kmf,
    s_g, s_gm, r_g, r_gm, s_z, r_z, s_f, r_f, s_l, beside,
):
    y = lax.axis_index("group")
    d = lax.axis_index("dev")
    x, z, c = d // (2 * NZ), (d // 2) % NZ, d % 2

    loads = [
        pltpu.make_async_copy(src, dst, s_in.at[n])
        for n, (src, dst) in enumerate(
            ((qry_hbm, qry_ref), (clu_hbm, clu_ref), (ord_hbm, ord_ref), (emb_hbm, emb_ref))
        )
    ]
    for load in loads:
        load.start()

    def peer(dy=0, dx=0, dz=0, dc=0):
        return (
            (y + dy) % NY,
            (((x + dx) % NX) * NZ + (z + dz) % NZ) * 2 + (c + dc) % 2,
        )

    def rcopy(src, dst, ssem, rsem, to):
        return pltpu.make_async_remote_copy(
            src_ref=src, dst_ref=dst, send_sem=ssem, recv_sem=rsem,
            device_id=to, device_id_type=MESH,
        )

    def by_core(x_then_z, z_then_x):
        pl.when(c == 1)(x_then_z)
        pl.when(c == 0)(z_then_x)

    barrier = pltpu.get_barrier_semaphore()
    X_PEERS = [dict(dz=1), dict(dz=-1)] + [dict(dy=k // NX, dx=k % NX) for k in range(1, NY * NX)]
    Z_PEERS = [dict(dz=1), dict(dz=-1)] + [dict(dx=k) for k in range(1, NX)]
    Z_PEERS += [dict(dy=k, dz=dz) for k in range(1, NY) for dz in (0, 1, -1)]

    def greet(peers):
        for to in peers:
            pl.semaphore_signal(barrier, inc=1, device_id=peer(**to), device_id_type=MESH)

    by_core(lambda: greet(X_PEERS), lambda: greet(Z_PEERS + [dict(dc=1)]))

    def unit_of(rows):
        wide = rows.astype(F32)
        total = jnp.sum(wide * wide, axis=-1, keepdims=True)
        return (wide * lax.rsqrt(total + 1e-06)).astype(BF16)

    for load in loads[:3]:
        load.wait()
    clu, order = clu_ref[...], ord_ref[...]
    row = iota((8, ROWS), 0)
    digits = jnp.where(
        row == 0,
        clu + 1,
        jnp.where(
            row == 1,
            order & 255,
            jnp.where(row == 2, (order >> 8) & 255, jnp.where(row == 3, order >> 16, 0)),
        ),
    ).astype(F32).astype(BF16)

    lanes = jnp.concatenate([qry_ref[...], qry_ref[...]], axis=1).astype(F32)
    column = jnp.transpose(jnp.broadcast_to(lanes, (128, 128)))[:QB]
    column = jnp.concatenate([column] * (ROWS // 128), axis=1)
    pick = jnp.where(column == iota((QB, ROWS), 1).astype(F32), 1.0, 0.0).astype(BF16)
    picked = lax.dot_general(digits, pick, (((1,), (1,)), ((), ())), preferred_element_type=F32)
    picked = meta_tile(jnp.concatenate([picked, picked], axis=1))
    lane = iota((8, 128), 1)
    for i in range(NY):
        tile = jnp.where((lane // RUN) % NY == i, picked, 0.0)
        tile = tile + pltpu.roll(tile, RUN, 1)
        qmsrc[i] = (tile + pltpu.roll(tile, 2 * RUN, 1))[0:2]
    loads[3].wait()
    qsel[...] = unit_of(jnp.dot(pick, emb_ref[...], preferred_element_type=F32))

    by_core(
        lambda: pl.semaphore_wait(barrier, len(X_PEERS) + 1),
        lambda: pl.semaphore_wait(barrier, len(Z_PEERS)),
    )

    @pl.when(c == 1)
    def _():
        pl.semaphore_signal(beside, inc=1, device_id=peer(dc=1), device_id_type=MESH)

    AT = {0: 0, -1: 1, 1: 2, -2: 3, 2: 4, -3: 5, 3: 6, 4: 7, -4: 7}

    def run_at(which):
        return pl.ds(pl.multiple_of(which * RUN, RUN), RUN)

    def block_at(at, xs, k=0, size=QB):
        return qbuf.at[pl.ds(pl.multiple_of(at * NX * QB + xs * QB + k * RUN, RUN), size)]

    sent = {"x": 0, "z": 0}

    def send(who, dx, source, target, to):
        xs = (x + dx) % NX
        n = sent[who]
        sent[who] += 1
        rcopy(block_at(source, xs), block_at(target, xs), s_g.at[n], r_g.at[target, xs], to).start()
        rcopy(qmeta.at[source, xs], qmeta.at[target, xs], s_gm.at[n], r_gm.at[target, xs], to).start()

    def along_z(who, dx, dz, step):
        send(who, dx, AT[dz], AT[dz - step], peer(dz=step))

    def along_x(dz):
        for dx in (1, 3, 2):
            send("z", 0, AT[dz], AT[dz], peer(dx=dx))

    def across(who, dx):
        t = 1 - 2 * (((x + dx) % NX) % 2)
        send(who, dx, 5 + (1 - t) // 2, 7, peer(dz=t))

    def arrive(dx, dz):
        at, xs = AT[dz], (x + dx) % NX
        rcopy(block_at(at, xs), block_at(at, xs), s_g.at[0], r_g.at[at, xs], peer(dc=1)).wait_recv()
        rcopy(qmeta.at[at, xs], qmeta.at[at, xs], s_gm.at[0], r_gm.at[at, xs], peer(dc=1)).wait_recv()

    X_RUNS = [(k, dx) for dx in (2, 1, 3, 0) for k in (2, 1, 3, 0) if (k, dx) != (0, 0)]
    Z_RUNS = [(k, dz) for dz in (1, -1, 0) for k in (2, 1, 3, 0) if (k, dz) != (0, 0)]

    def run_send(n, k, at, slot, to):
        i, back = (y + k) % NY, (NY - k) % NY
        rcopy(qsel.at[run_at(i)], block_at(at, x, back, RUN), s_q.at[n], r_q.at[slot, back], to).start()
        rcopy(qmsrc.at[i], qmrecv.at[slot, back], s_m.at[n], r_m.at[slot, back], to).start()

    def runs_arrive(at, xs, slot, own):
        for k in (0, 1, 3, 2)[own:]:
            rcopy(qsel.at[pl.ds(0, RUN)], block_at(at, xs, k, RUN), s_q.at[0], r_q.at[slot, k], peer(dc=1)).wait_recv()
            rcopy(qmsrc.at[0], qmrecv.at[slot, k], s_m.at[0], r_m.at[slot, k], peer(dc=1)).wait_recv()
        tile = qmrecv[slot, 0]
        for k in range(1, NY):
            tile = jnp.where((lane[0:2] // RUN) % NY == k, qmrecv[slot, k], tile)
        qmeta[at, xs] = tile

    def x_runs():
        for n, (k, dx) in enumerate(X_RUNS):
            run_send(n, k, 0, x, peer(dy=k, dx=dx))
        qmrecv[x, 0] = qmsrc[y]

    def z_runs():
        for n, (k, dz) in enumerate(Z_RUNS):
            run_send(n, k, AT[-dz], AT[-dz], peer(dy=k, dz=dz))
        qmrecv[0, 0] = qmsrc[y]

    by_core(x_runs, z_runs)
    block_at(0, x, 0, RUN)[...] = qsel[run_at(y)]

    unit[...] = unit_of(emb_ref[...])
    residue = clu % NY
    member = jnp.where(row == residue, 1.0, 0.0)
    before = jnp.where(iota((ROWS, ROWS), 0) < iota((ROWS, ROWS), 1), 1.0, 0.0).astype(BF16)
    prefix = jnp.dot(member.astype(BF16), before, preferred_element_type=F32)
    rank = jnp.sum(member * prefix, axis=0, keepdims=True)
    dest = residue.astype(F32) * CAP + rank
    slot_of = iota((CAP, ROWS), 0)

    def of_residue(r):
        place = jnp.where((slot_of + r * CAP).astype(F32) == dest, 1.0, 0.0).astype(BF16)
        rows = jnp.dot(place, unit[...], preferred_element_type=F32).astype(BF16)
        tile = lax.dot_general(digits, place, (((1,), (1,)), ((), ())), preferred_element_type=F32)
        return rows, meta_tile(tile)[0:2]

    PLACE = {0: 0, 1: 1, 3: 2, 2: 3}

    def key_at(j, cs):
        return kbuf.at[pl.ds(pl.multiple_of(j * 2 * CAP + cs * CAP, CAP), CAP)]

    def key_send(k):
        j, to = PLACE[k], peer(dy=k)
        rcopy(ksel.at[k], key_at(j, c), s_k.at[k], r_k.at[j, c], to).start()
        rcopy(kmsrc.at[k], kmeta.at[j, c], s_km.at[k], r_km.at[j, c], to).start()

    def key_wait(j, cs):
        rcopy(key_at(j, cs), key_at(j, cs), s_kf.at[0], r_k.at[j, cs], peer(dc=1)).wait_recv()
        rcopy(kmeta.at[j, cs], kmeta.at[j, cs], s_kmf.at[0], r_km.at[j, cs], peer(dc=1)).wait_recv()

    def key_share(j):
        rcopy(key_at(j, c), key_at(j, c), s_kf.at[j], r_k.at[j, c], peer(dc=1)).start()
        rcopy(kmeta.at[j, c], kmeta.at[j, c], s_kmf.at[j], r_km.at[j, c], peer(dc=1)).start()

    def key_codes(j):
        for cs in range(2):
            tile = kmeta[j, cs]
            code = (tile[0:1] - 1.0) * SPAN + tile[1:2]
            at = (j * 2 + cs) * CAP
            kcode[at:at + CAP, :] = jnp.transpose(jnp.broadcast_to(code, (128, CAP)))

    for k in (1, 3, 2):
        rows, tile = of_residue((y + k) % NY)
        ksel[k] = rows
        kmsrc[k] = tile
        key_send(k)
    rows, tile = of_residue(y)
    kbuf[pl.ds(pl.multiple_of(c * CAP, CAP), CAP)] = rows
    kmeta[0, c] = tile

    def x_start():
        for dx in (0, 1, 3, 2):
            xs = (x + dx) % NX
            runs_arrive(0, xs, xs, int(dx == 0))
            for step in (1, -1):
                along_z("x", dx, 0, step)

    def x_step(s):
        for dx in (0, 1, 3, 2):
            if s == 4:
                arrive(dx, 4)
                continue
            for dz in (-s, s):
                arrive(dx, dz)
                if s < 3:
                    along_z("x", dx, dz, 1 if dz < 0 else -1)
            if s == 3:
                across("x", dx)

    def z_start():
        for dz in (-1, 1, 0):
            runs_arrive(AT[dz], x, AT[dz], int(dz == 0))
            if dz != 0:
                along_z("z", 0, dz, -dz)
        for dz in (0, -1, 1):
            along_x(dz)

    def z_step(s):
        if s == 4:
            arrive(0, 4)
            along_x(4)
            return
        for dz in (-s, s):
            arrive(0, dz)
            if s < 3:
                along_z("z", 0, dz, 1 if dz < 0 else -1)
        if s == 3:
            across("z", 0)
        for dz in (-s, s):
            along_x(dz)

    def x_wait(s):
        for dz in ((s,) if s in (0, 4) else (-s, s)):
            for dx in (1, 3, 2):
                arrive(dx, dz)

    def rect(i0, i1, j0, j1):
        first, last = j0 * 2 * CAP, j1 * 2 * CAP
        s = lax.dot_general(
            kbuf[first:last], qbuf[i0 * NX * QB:i1 * NX * QB],
            (((1,), (1,)), ((), ())), preferred_element_type=F32,
        )
        code = kcode[first:last]
        for i in range(i0, i1):
            for p in range(2):
                tile = jnp.where(lane[0:2] < QB, qmeta[i, 2 * p], qmeta[i, 2 * p + 1])
                low = (tile[0:1] - 1.0) * SPAN
                high = low + tile[1:2]
                keep = (code >= low) & (code < high)
                at = ((i - i0) * 2 + p) * 128
                top = jnp.max(jnp.where(keep, s[:, at:at + 128], -1.0), axis=0, keepdims=True)
                best[i, p:p + 1, :] = jnp.maximum(best[i, p:p + 1, :], top)

    FAR = (0, -1, 1, -2, 2, -3, 3, 4)

    def slab_copy(i):
        return rcopy(best.at[i], zred.at[i], s_z.at[i], r_z.at[i], peer(dz=FAR[i]))

    HOME = [(k, dx) for dx in (2, 1, 3, 0) for k in (2, 1, 3, 0)]

    def home_copy(n, across):
        k, dx = HOME[n]
        if across:
            return rcopy(best.at[7], fin.at[1, y, x], s_l.at[n], r_f.at[1, y, x], peer(dy=k, dx=dx, dz=4))
        return rcopy(rtile, fin.at[0, y, x], s_f.at[n], r_f.at[0, y, x], peer(dy=k, dx=dx))

    best[...] = jnp.full(best.shape, -1.0, F32)

    def both(*steps):
        for step in steps:
            step()

    by_core(x_start, lambda: both(z_start, lambda: x_wait(0)))

    @pl.when(c == 0)
    def _():
        pl.semaphore_wait(beside, 1)

    key_share(0)
    key_wait(0, 1 - c)
    key_codes(0)
    rect(0, 1, 0, 1)
    by_core(lambda: x_step(1), lambda: both(lambda: z_step(2), lambda: x_wait(1)))
    rect(1, 3, 0, 1)
    for j in (1, 2):
        key_wait(j, c)
        key_share(j)
    by_core(lambda: x_step(2), lambda: both(lambda: z_step(3), lambda: x_wait(2), lambda: z_step(4)))
    for j in (1, 2):
        key_wait(j, 1 - c)
        key_codes(j)
    rect(0, 3, 1, 3)
    rect(3, 5, 0, 3)
    by_core(lambda: x_step(3), lambda: x_wait(3))
    rect(5, 7, 0, 3)
    key_wait(3, c)
    key_share(3)
    key_wait(3, 1 - c)
    key_codes(3)
    rect(0, 7, 3, 4)
    for i in range(1, 7):
        slab_copy(i).start()
    by_core(lambda: x_step(4), lambda: x_wait(4))
    rect(7, 8, 0, 4)

    for n in range(len(HOME)):
        home_copy(n, True).start()
    top = best[0]
    for i in range(1, 7):
        slab_copy(i).wait_recv()
        top = jnp.maximum(top, zred[i])
    rtile[...] = top
    for n in range(len(HOME) - 1):
        home_copy(n, False).start()
    fin[0, y, x] = top
    for k, dx in reversed(HOME):
        ys, xs = (y + k) % NY, (x + dx) % NX
        for q in range(2):
            if q == 1 or (k, dx) != (0, 0):
                rcopy(rtile, fin.at[q, ys, xs], s_f.at[0], r_f.at[q, ys, xs], peer(dc=1)).wait_recv()
    result = jnp.zeros((8, 128), F32)
    for r in range(NY):
        tile = jnp.max(fin[:, r].reshape(2 * NX, 2, 128), axis=0)
        tile = jnp.where(x // 2 == 0, tile[0:1], tile[1:2])
        tile = jnp.broadcast_to(tile, (8, 128))
        tile = pltpu.roll(tile, (r * RUN - (x % 2) * QB - ((y - r + NY) % NY) * RUN + 256) % 128, 1)
        result = jnp.where(lane // RUN == r, tile, result)
    out_ref[...] = result[0, 0:QB]

    def drain(runs, count):
        for n in range(runs):
            rcopy(qsel.at[pl.ds(0, RUN)], block_at(0, x, 0, RUN), s_q.at[n], r_q.at[0, 0], peer(dc=1)).wait_send()
            rcopy(qmsrc.at[0], qmrecv.at[0, 0], s_m.at[n], r_m.at[0, 0], peer(dc=1)).wait_send()
        for n in range(count):
            rcopy(block_at(0, x), block_at(0, x), s_g.at[n], r_g.at[0, x], peer(dc=1)).wait_send()
            rcopy(qmeta.at[0, x], qmeta.at[0, x], s_gm.at[n], r_gm.at[0, x], peer(dc=1)).wait_send()

    by_core(lambda: drain(len(X_RUNS), sent["x"]), lambda: drain(len(Z_RUNS), sent["z"]))
    for k in range(1, NY):
        rcopy(ksel.at[k], key_at(0, c), s_k.at[k], r_k.at[0, c], peer(dy=k)).wait_send()
        rcopy(kmsrc.at[k], kmeta.at[0, c], s_km.at[k], r_km.at[0, c], peer(dy=k)).wait_send()
    for j in range(NY):
        rcopy(key_at(j, c), key_at(j, c), s_kf.at[j], r_k.at[j, c], peer(dc=1)).wait_send()
        rcopy(kmeta.at[j, c], kmeta.at[j, c], s_kmf.at[j], r_km.at[j, c], peer(dc=1)).wait_send()
    for i in range(1, 7):
        slab_copy(i).wait_send()
    for n in range(len(HOME)):
        home_copy(n, True).wait_send()
        if n < len(HOME) - 1:
            home_copy(n, False).wait_send()


def body(embeddings, cluster, order, query_local):
    dma = pltpu.SemaphoreType.DMA
    out = pl.pallas_call(
        kernel,
        out_shape=jax.ShapeDtypeStruct((QB,), F32),
        in_specs=[pl.BlockSpec(memory_space=pl.ANY)] * 4,
        out_specs=pl.BlockSpec(memory_space=pltpu.VMEM),
        scratch_shapes=[
            pltpu.VMEM((ROWS, D), BF16),
            pltpu.VMEM((1, ROWS), jnp.int32),
            pltpu.VMEM((1, ROWS), jnp.int32),
            pltpu.VMEM((1, QB), jnp.int32),
            pltpu.VMEM((ROWS, D), BF16),
            pltpu.VMEM((QB, D), BF16),
            pltpu.VMEM((NY, 2, 128), F32),
            pltpu.VMEM((NX, NY, 2, 128), F32),
            pltpu.VMEM((NY, CAP, D), BF16),
            pltpu.VMEM((NY, 2, CAP), F32),
            pltpu.VMEM((NY * 2 * CAP, D), BF16),
            pltpu.VMEM((NY, 2, 2, CAP), F32),
            pltpu.VMEM((NY * 2 * CAP, 128), F32),
            pltpu.VMEM((NZ * NX * QB, D), BF16),
            pltpu.VMEM((NZ, NX, 2, 128), F32),
            pltpu.VMEM((NZ, 2, 128), F32),
            pltpu.VMEM((NZ, 2, 128), F32),
            pltpu.VMEM((2, 128), F32),
            pltpu.VMEM((2, NY, NX, 2, 128), F32),
            dma((4,)), dma((15,)), dma((15,)), dma((NX, NY)), dma((NX, NY)),
            dma((NY,)), dma((NY,)), dma((NY, 2)), dma((NY, 2)), dma((NY,)), dma((NY,)),
            dma((29,)), dma((29,)), dma((NZ, NX)), dma((NZ, NX)),
            dma((NZ,)), dma((NZ,)), dma((NY * NX,)), dma((2, NY, NX)), dma((NY * NX,)),
            pltpu.SemaphoreType.REGULAR,
        ],
        compiler_params=pltpu.CompilerParams(
            collective_id=0, has_side_effects=True, vmem_limit_bytes=56 * 1024 * 1024
        ),
        name="dedup",
    )(
        embeddings,
        cluster.reshape(1, ROWS),
        order.reshape(1, ROWS),
        query_local.reshape(1, QB),
    )
    return out


def solution(mesh):
    return jax.shard_map(
        body,
        mesh=mesh,
        in_specs=(
            P(("group", "dev"), None),
            P(("group", "dev")),
            P(("group", "dev")),
            P(("group", "dev")),
        ),
        out_specs=P(("group", "dev")),
        check_vma=False,
    )
```

```python
import jax
import jax.numpy as jnp
from jax import lax
from jax.experimental import pallas as pl
from jax.experimental.pallas import tpu as pltpu
from jax.sharding import PartitionSpec as P

MESH = pl.DeviceIdType.MESH
F32, BF16 = jnp.float32, jnp.bfloat16
NY, NX, NZ = 4, 4, 8
D = 768
ROWS = 512
QB = 64
RUN = 16
CAP = 256
SPAN = 131072.0


def iota(shape, axis):
    return lax.broadcasted_iota(jnp.int32, shape, axis)


def meta_tile(picked):
    order = picked[1:2] + 256.0 * picked[2:3] + 65536.0 * picked[3:4]
    return jnp.where(iota(picked.shape, 0) == 0, picked[0:1], order)


def kernel(
    emb_hbm, clu_hbm, ord_hbm, qry_hbm, out_ref,
    emb_ref, clu_ref, ord_ref, qry_ref,
    unit, qsel, qmsrc, qmrecv, ksel, kmsrc, kbuf, kmeta, kcode, qbuf, qmeta,
    best, zred, rtile, fin,
    s_in, s_q, s_m, r_q, r_m, s_k, s_km, r_k, r_km, s_kf, s_kmf,
    s_g, s_gm, r_g, r_gm, s_z, r_z, s_f, r_f, s_l, beside,
):
    y = lax.axis_index("group")
    d = lax.axis_index("dev")
    x, z, c = d // (2 * NZ), (d // 2) % NZ, d % 2

    loads = [
        pltpu.make_async_copy(src, dst, s_in.at[n])
        for n, (src, dst) in enumerate(
            ((qry_hbm, qry_ref), (clu_hbm, clu_ref), (ord_hbm, ord_ref), (emb_hbm, emb_ref))
        )
    ]
    for load in loads:
        load.start()

    def peer(dy=0, dx=0, dz=0, dc=0):
        return (
            (y + dy) % NY,
            (((x + dx) % NX) * NZ + (z + dz) % NZ) * 2 + (c + dc) % 2,
        )

    def rcopy(src, dst, ssem, rsem, to):
        return pltpu.make_async_remote_copy(
            src_ref=src, dst_ref=dst, send_sem=ssem, recv_sem=rsem,
            device_id=to, device_id_type=MESH,
        )

    def by_core(x_then_z, z_then_x):
        pl.when(c == 1)(x_then_z)
        pl.when(c == 0)(z_then_x)

    barrier = pltpu.get_barrier_semaphore()
    X_PEERS = [dict(dz=1), dict(dz=-1)] + [dict(dy=k // NX, dx=k % NX) for k in range(1, NY * NX)]
    Z_PEERS = [dict(dz=1), dict(dz=-1)] + [dict(dx=k) for k in range(1, NX)]
    Z_PEERS += [dict(dy=k, dz=dz) for k in range(1, NY) for dz in (0, 1, -1)]

    def greet(peers):
        for to in peers:
            pl.semaphore_signal(barrier, inc=1, device_id=peer(**to), device_id_type=MESH)

    by_core(lambda: greet(X_PEERS), lambda: greet(Z_PEERS + [dict(dc=1)]))

    def unit_of(rows):
        wide = rows.astype(F32)
        total = jnp.sum(wide * wide, axis=-1, keepdims=True)
        return (wide * lax.rsqrt(total + 1e-06)).astype(BF16)

    for load in loads[:3]:
        load.wait()
    clu, order = clu_ref[...], ord_ref[...]
    row = iota((8, ROWS), 0)
    digits = jnp.where(
        row == 0,
        clu + 1,
        jnp.where(
            row == 1,
            order & 255,
            jnp.where(row == 2, (order >> 8) & 255, jnp.where(row == 3, order >> 16, 0)),
        ),
    ).astype(F32).astype(BF16)

    lanes = jnp.concatenate([qry_ref[...], qry_ref[...]], axis=1).astype(F32)
    column = jnp.transpose(jnp.broadcast_to(lanes, (128, 128)))[:QB]
    column = jnp.concatenate([column] * (ROWS // 128), axis=1)
    pick = jnp.where(column == iota((QB, ROWS), 1).astype(F32), 1.0, 0.0).astype(BF16)
    picked = lax.dot_general(digits, pick, (((1,), (1,)), ((), ())), preferred_element_type=F32)
    picked = meta_tile(jnp.concatenate([picked, picked], axis=1))
    lane = iota((8, 128), 1)
    for i in range(NY):
        tile = jnp.where((lane // RUN) % NY == i, picked, 0.0)
        tile = tile + pltpu.roll(tile, RUN, 1)
        qmsrc[i] = (tile + pltpu.roll(tile, 2 * RUN, 1))[0:2]
    loads[3].wait()
    qsel[...] = unit_of(jnp.dot(pick, emb_ref[...], preferred_element_type=F32))

    by_core(
        lambda: pl.semaphore_wait(barrier, len(X_PEERS) + 1),
        lambda: pl.semaphore_wait(barrier, len(Z_PEERS)),
    )

    @pl.when(c == 1)
    def _():
        pl.semaphore_signal(beside, inc=1, device_id=peer(dc=1), device_id_type=MESH)

    AT = {0: 0, -1: 1, 1: 2, -2: 3, 2: 4, -3: 5, 3: 6, 4: 7, -4: 7}

    def run_at(which):
        return pl.ds(pl.multiple_of(which * RUN, RUN), RUN)

    def block_at(at, xs, k=0, size=QB):
        return qbuf.at[pl.ds(pl.multiple_of(at * NX * QB + xs * QB + k * RUN, RUN), size)]

    sent = {"x": 0, "z": 0}

    def send(who, dx, source, target, to):
        xs = (x + dx) % NX
        n = sent[who]
        sent[who] += 1
        rcopy(block_at(source, xs), block_at(target, xs), s_g.at[n], r_g.at[target, xs], to).start()
        rcopy(qmeta.at[source, xs], qmeta.at[target, xs], s_gm.at[n], r_gm.at[target, xs], to).start()

    def along_z(who, dx, dz, step):
        send(who, dx, AT[dz], AT[dz - step], peer(dz=step))

    def along_x(dz):
        for dx in (1, 3, 2):
            send("z", 0, AT[dz], AT[dz], peer(dx=dx))

    def across(who, dx):
        t = 1 - 2 * (((x + dx) % NX) % 2)
        send(who, dx, 5 + (1 - t) // 2, 7, peer(dz=t))

    def arrive(dx, dz):
        at, xs = AT[dz], (x + dx) % NX
        rcopy(block_at(at, xs), block_at(at, xs), s_g.at[0], r_g.at[at, xs], peer(dc=1)).wait_recv()
        rcopy(qmeta.at[at, xs], qmeta.at[at, xs], s_gm.at[0], r_gm.at[at, xs], peer(dc=1)).wait_recv()

    X_RUNS = [(k, dx) for dx in (0, 1, 3, 2) for k in (2, 1, 3, 0) if (k, dx) != (0, 0)]
    Z_RUNS = [(k, dz) for dz in (0, 1, -1) for k in (2, 1, 3, 0) if (k, dz) != (0, 0)]

    def run_send(n, k, at, slot, to):
        i, back = (y + k) % NY, (NY - k) % NY
        rcopy(qsel.at[run_at(i)], block_at(at, x, back, RUN), s_q.at[n], r_q.at[slot, back], to).start()
        rcopy(qmsrc.at[i], qmrecv.at[slot, back], s_m.at[n], r_m.at[slot, back], to).start()

    def runs_arrive(at, xs, slot, own):
        for k in (0, 1, 3, 2)[own:]:
            rcopy(qsel.at[pl.ds(0, RUN)], block_at(at, xs, k, RUN), s_q.at[0], r_q.at[slot, k], peer(dc=1)).wait_recv()
            rcopy(qmsrc.at[0], qmrecv.at[slot, k], s_m.at[0], r_m.at[slot, k], peer(dc=1)).wait_recv()
        tile = qmrecv[slot, 0]
        for k in range(1, NY):
            tile = jnp.where((lane[0:2] // RUN) % NY == k, qmrecv[slot, k], tile)
        qmeta[at, xs] = tile

    def x_runs():
        for n, (k, dx) in enumerate(X_RUNS):
            run_send(n, k, 0, x, peer(dy=k, dx=dx))
        qmrecv[x, 0] = qmsrc[y]

    def z_runs():
        for n, (k, dz) in enumerate(Z_RUNS):
            run_send(n, k, AT[-dz], AT[-dz], peer(dy=k, dz=dz))
        qmrecv[0, 0] = qmsrc[y]

    by_core(x_runs, z_runs)
    block_at(0, x, 0, RUN)[...] = qsel[run_at(y)]

    unit[...] = unit_of(emb_ref[...])
    residue = clu % NY
    member = jnp.where(row == residue, 1.0, 0.0)
    before = jnp.where(iota((ROWS, ROWS), 0) < iota((ROWS, ROWS), 1), 1.0, 0.0).astype(BF16)
    prefix = jnp.dot(member.astype(BF16), before, preferred_element_type=F32)
    rank = jnp.sum(member * prefix, axis=0, keepdims=True)
    dest = residue.astype(F32) * CAP + rank
    slot_of = iota((CAP, ROWS), 0)

    def of_residue(r):
        place = jnp.where((slot_of + r * CAP).astype(F32) == dest, 1.0, 0.0).astype(BF16)
        rows = jnp.dot(place, unit[...], preferred_element_type=F32).astype(BF16)
        tile = lax.dot_general(digits, place, (((1,), (1,)), ((), ())), preferred_element_type=F32)
        return rows, meta_tile(tile)[0:2]

    PLACE = {0: 0, 1: 1, 3: 2, 2: 3}

    def key_at(j, cs):
        return kbuf.at[pl.ds(pl.multiple_of(j * 2 * CAP + cs * CAP, CAP), CAP)]

    def key_send(k):
        j, to = PLACE[k], peer(dy=k)
        rcopy(ksel.at[k], key_at(j, c), s_k.at[k], r_k.at[j, c], to).start()
        rcopy(kmsrc.at[k], kmeta.at[j, c], s_km.at[k], r_km.at[j, c], to).start()

    def key_wait(j, cs):
        rcopy(key_at(j, cs), key_at(j, cs), s_kf.at[0], r_k.at[j, cs], peer(dc=1)).wait_recv()
        rcopy(kmeta.at[j, cs], kmeta.at[j, cs], s_kmf.at[0], r_km.at[j, cs], peer(dc=1)).wait_recv()

    def key_share(j):
        rcopy(key_at(j, c), key_at(j, c), s_kf.at[j], r_k.at[j, c], peer(dc=1)).start()
        rcopy(kmeta.at[j, c], kmeta.at[j, c], s_kmf.at[j], r_km.at[j, c], peer(dc=1)).start()

    def key_codes(j):
        for cs in range(2):
            tile = kmeta[j, cs]
            code = (tile[0:1] - 1.0) * SPAN + tile[1:2]
            at = (j * 2 + cs) * CAP
            kcode[at:at + CAP, :] = jnp.transpose(jnp.broadcast_to(code, (128, CAP)))

    for k in (1, 3, 2):
        rows, tile = of_residue((y + k) % NY)
        ksel[k] = rows
        kmsrc[k] = tile
        key_send(k)
    rows, tile = of_residue(y)
    kbuf[pl.ds(pl.multiple_of(c * CAP, CAP), CAP)] = rows
    kmeta[0, c] = tile

    def x_start():
        for dx in (0, 1, 3, 2):
            xs = (x + dx) % NX
            runs_arrive(0, xs, xs, int(dx == 0))
            for step in (1, -1):
                along_z("x", dx, 0, step)

    def x_step(s):
        for dx in (0, 1, 3, 2):
            if s == 4:
                arrive(dx, 4)
                continue
            for dz in (-s, s):
                arrive(dx, dz)
                if s < 3:
                    along_z("x", dx, dz, 1 if dz < 0 else -1)
            if s == 3:
                across("x", dx)

    def z_start():
        for dz in (0, -1, 1):
            runs_arrive(AT[dz], x, AT[dz], int(dz == 0))
            if dz == 0:
                along_x(0)
            if dz != 0:
                along_z("z", 0, dz, -dz)
        for dz in (-1, 1):
            along_x(dz)

    def z_step(s):
        if s == 4:
            arrive(0, 4)
            along_x(4)
            return
        for dz in (-s, s):
            arrive(0, dz)
            if s < 3:
                along_z("z", 0, dz, 1 if dz < 0 else -1)
        if s == 3:
            across("z", 0)
        for dz in (-s, s):
            along_x(dz)

    def x_wait(s):
        for dz in ((s,) if s in (0, 4) else (-s, s)):
            for dx in (1, 3, 2):
                arrive(dx, dz)

    def rect(i0, i1, j0, j1):
        first, last = j0 * 2 * CAP, j1 * 2 * CAP
        s = lax.dot_general(
            kbuf[first:last], qbuf[i0 * NX * QB:i1 * NX * QB],
            (((1,), (1,)), ((), ())), preferred_element_type=F32,
        )
        code = kcode[first:last]
        for i in range(i0, i1):
            for p in range(2):
                tile = jnp.where(lane[0:2] < QB, qmeta[i, 2 * p], qmeta[i, 2 * p + 1])
                low = (tile[0:1] - 1.0) * SPAN
                high = low + tile[1:2]
                keep = (code >= low) & (code < high)
                at = ((i - i0) * 2 + p) * 128
                top = jnp.max(jnp.where(keep, s[:, at:at + 128], -1.0), axis=0, keepdims=True)
                best[i, p:p + 1, :] = jnp.maximum(best[i, p:p + 1, :], top)

    FAR = (0, -1, 1, -2, 2, -3, 3, 4)

    def slab_copy(i):
        return rcopy(best.at[i], zred.at[i], s_z.at[i], r_z.at[i], peer(dz=FAR[i]))

    HOME = [(k, dx) for dx in (2, 1, 3, 0) for k in (2, 1, 3, 0)]

    def home_copy(n, across):
        k, dx = HOME[n]
        if across:
            return rcopy(best.at[7], fin.at[1, y, x], s_l.at[n], r_f.at[1, y, x], peer(dy=k, dx=dx, dz=4))
        return rcopy(rtile, fin.at[0, y, x], s_f.at[n], r_f.at[0, y, x], peer(dy=k, dx=dx))

    best[...] = jnp.full(best.shape, -1.0, F32)

    def both(*steps):
        for step in steps:
            step()

    by_core(x_start, lambda: both(z_start, lambda: z_step(2), lambda: x_wait(0)))

    @pl.when(c == 0)
    def _():
        pl.semaphore_wait(beside, 1)

    key_share(0)
    key_wait(0, 1 - c)
    key_codes(0)
    rect(0, 1, 0, 1)
    by_core(lambda: x_step(1), lambda: both(lambda: z_step(3), lambda: x_wait(1)))
    rect(1, 3, 0, 1)
    for j in (1, 2):
        key_wait(j, c)
        key_share(j)
    by_core(lambda: x_step(2), lambda: both(lambda: z_step(4), lambda: x_wait(2)))
    for j in (1, 2):
        key_wait(j, 1 - c)
        key_codes(j)
    rect(0, 3, 1, 3)
    rect(3, 5, 0, 3)
    by_core(lambda: x_step(3), lambda: None)
    key_wait(3, c)
    key_share(3)
    by_core(lambda: None, lambda: x_wait(3))
    rect(5, 7, 0, 3)
    key_wait(3, 1 - c)
    key_codes(3)
    rect(0, 7, 3, 4)
    for i in range(1, 7):
        slab_copy(i).start()
    by_core(lambda: x_step(4), lambda: x_wait(4))
    rect(7, 8, 0, 4)

    for n in range(len(HOME)):
        home_copy(n, True).start()
    top = best[0]
    for i in range(1, 7):
        slab_copy(i).wait_recv()
        top = jnp.maximum(top, zred[i])
    rtile[...] = top
    for n in range(len(HOME) - 1):
        home_copy(n, False).start()
    def drain(runs, count):
        for n in range(runs):
            rcopy(qsel.at[pl.ds(0, RUN)], block_at(0, x, 0, RUN), s_q.at[n], r_q.at[0, 0], peer(dc=1)).wait_send()
            rcopy(qmsrc.at[0], qmrecv.at[0, 0], s_m.at[n], r_m.at[0, 0], peer(dc=1)).wait_send()
        for n in range(count):
            rcopy(block_at(0, x), block_at(0, x), s_g.at[n], r_g.at[0, x], peer(dc=1)).wait_send()
            rcopy(qmeta.at[0, x], qmeta.at[0, x], s_gm.at[n], r_gm.at[0, x], peer(dc=1)).wait_send()

    by_core(lambda: drain(len(X_RUNS), sent["x"]), lambda: drain(len(Z_RUNS), sent["z"]))
    for k in range(1, NY):
        rcopy(ksel.at[k], key_at(0, c), s_k.at[k], r_k.at[0, c], peer(dy=k)).wait_send()
        rcopy(kmsrc.at[k], kmeta.at[0, c], s_km.at[k], r_km.at[0, c], peer(dy=k)).wait_send()
    for j in range(NY):
        rcopy(key_at(j, c), key_at(j, c), s_kf.at[j], r_k.at[j, c], peer(dc=1)).wait_send()
        rcopy(kmeta.at[j, c], kmeta.at[j, c], s_kmf.at[j], r_km.at[j, c], peer(dc=1)).wait_send()
    for i in range(1, 7):
        slab_copy(i).wait_send()
    fin[0, y, x] = top
    for k, dx in reversed(HOME):
        ys, xs = (y + k) % NY, (x + dx) % NX
        for q in range(2):
            if q == 1 or (k, dx) != (0, 0):
                rcopy(rtile, fin.at[q, ys, xs], s_f.at[0], r_f.at[q, ys, xs], peer(dc=1)).wait_recv()
    result = jnp.zeros((8, 128), F32)
    for r in range(NY):
        tile = jnp.max(fin[:, r].reshape(2 * NX, 2, 128), axis=0)
        tile = jnp.where(x // 2 == 0, tile[0:1], tile[1:2])
        tile = jnp.broadcast_to(tile, (8, 128))
        tile = pltpu.roll(tile, (r * RUN - (x % 2) * QB - ((y - r + NY) % NY) * RUN + 256) % 128, 1)
        result = jnp.where(lane // RUN == r, tile, result)
    out_ref[...] = result[0, 0:QB]

    for n in range(len(HOME)):
        home_copy(n, True).wait_send()
        if n < len(HOME) - 1:
            home_copy(n, False).wait_send()


def body(embeddings, cluster, order, query_local):
    dma = pltpu.SemaphoreType.DMA
    out = pl.pallas_call(
        kernel,
        out_shape=jax.ShapeDtypeStruct((QB,), F32),
        in_specs=[pl.BlockSpec(memory_space=pl.ANY)] * 4,
        out_specs=pl.BlockSpec(memory_space=pltpu.VMEM),
        scratch_shapes=[
            pltpu.VMEM((ROWS, D), BF16),
            pltpu.VMEM((1, ROWS), jnp.int32),
            pltpu.VMEM((1, ROWS), jnp.int32),
            pltpu.VMEM((1, QB), jnp.int32),
            pltpu.VMEM((ROWS, D), BF16),
            pltpu.VMEM((QB, D), BF16),
            pltpu.VMEM((NY, 2, 128), F32),
            pltpu.VMEM((NX, NY, 2, 128), F32),
            pltpu.VMEM((NY, CAP, D), BF16),
            pltpu.VMEM((NY, 2, CAP), F32),
            pltpu.VMEM((NY * 2 * CAP, D), BF16),
            pltpu.VMEM((NY, 2, 2, CAP), F32),
            pltpu.VMEM((NY * 2 * CAP, 128), F32),
            pltpu.VMEM((NZ * NX * QB, D), BF16),
            pltpu.VMEM((NZ, NX, 2, 128), F32),
            pltpu.VMEM((NZ, 2, 128), F32),
            pltpu.VMEM((NZ, 2, 128), F32),
            pltpu.VMEM((2, 128), F32),
            pltpu.VMEM((2, NY, NX, 2, 128), F32),
            dma((4,)), dma((15,)), dma((15,)), dma((NX, NY)), dma((NX, NY)),
            dma((NY,)), dma((NY,)), dma((NY, 2)), dma((NY, 2)), dma((NY,)), dma((NY,)),
            dma((29,)), dma((29,)), dma((NZ, NX)), dma((NZ, NX)),
            dma((NZ,)), dma((NZ,)), dma((NY * NX,)), dma((2, NY, NX)), dma((NY * NX,)),
            pltpu.SemaphoreType.REGULAR,
        ],
        compiler_params=pltpu.CompilerParams(
            collective_id=0, has_side_effects=True, vmem_limit_bytes=56 * 1024 * 1024
        ),
        name="dedup",
    )(
        embeddings,
        cluster.reshape(1, ROWS),
        order.reshape(1, ROWS),
        query_local.reshape(1, QB),
    )
    return out


def solution(mesh):
    return jax.shard_map(
        body,
        mesh=mesh,
        in_specs=(
            P(("group", "dev"), None),
            P(("group", "dev")),
            P(("group", "dev")),
            P(("group", "dev")),
        ),
        out_specs=P(("group", "dev")),
        check_vma=False,
    )
```

```python
import jax
import jax.numpy as jnp
from jax import lax
from jax.experimental import pallas as pl
from jax.experimental.pallas import tpu as pltpu
from jax.sharding import PartitionSpec as P

MESH = pl.DeviceIdType.MESH
F32, BF16 = jnp.float32, jnp.bfloat16
NY, NX, NZ = 4, 4, 8
D = 768
ROWS = 512
QB = 64
RUN = 16
CAP = 256
SPAN = 131072.0


def iota(shape, axis):
    return lax.broadcasted_iota(jnp.int32, shape, axis)


def meta_tile(picked):
    order = picked[1:2] + 256.0 * picked[2:3] + 65536.0 * picked[3:4]
    return jnp.where(iota(picked.shape, 0) == 0, picked[0:1], order)


def kernel(
    emb_hbm, clu_hbm, ord_hbm, qry_hbm, out_ref,
    emb_ref, clu_ref, ord_ref, qry_ref,
    unit, qsel, qmsrc, qmrecv, ksel, kmsrc, kbuf, kmeta, kcode, qbuf, qmeta,
    best, zred, rtile, fin,
    s_in, s_q, s_m, r_q, r_m, s_k, s_km, r_k, r_km, s_kf, s_kmf,
    s_g, s_gm, r_g, r_gm, s_z, r_z, s_f, r_f, s_l, beside,
):
    y = lax.axis_index("group")
    d = lax.axis_index("dev")
    x, z, c = d // (2 * NZ), (d // 2) % NZ, d % 2

    loads = [
        pltpu.make_async_copy(src, dst, s_in.at[n])
        for n, (src, dst) in enumerate(
            ((qry_hbm, qry_ref), (clu_hbm, clu_ref), (ord_hbm, ord_ref), (emb_hbm, emb_ref))
        )
    ]
    for load in loads:
        load.start()

    def peer(dy=0, dx=0, dz=0, dc=0):
        return (
            (y + dy) % NY,
            (((x + dx) % NX) * NZ + (z + dz) % NZ) * 2 + (c + dc) % 2,
        )

    def rcopy(src, dst, ssem, rsem, to):
        return pltpu.make_async_remote_copy(
            src_ref=src, dst_ref=dst, send_sem=ssem, recv_sem=rsem,
            device_id=to, device_id_type=MESH,
        )

    def by_core(x_then_z, z_then_x):
        pl.when(c == 1)(x_then_z)
        pl.when(c == 0)(z_then_x)

    barrier = pltpu.get_barrier_semaphore()
    X_PEERS = [dict(dz=1), dict(dz=-1)] + [dict(dy=k // NX, dx=k % NX) for k in range(1, NY * NX)]
    Z_PEERS = [dict(dz=1), dict(dz=-1)] + [dict(dx=k) for k in range(1, NX)]
    Z_PEERS += [dict(dy=k, dz=dz) for k in range(1, NY) for dz in (0, 1, -1)]

    def greet(peers):
        for to in peers:
            pl.semaphore_signal(barrier, inc=1, device_id=peer(**to), device_id_type=MESH)

    by_core(lambda: greet(X_PEERS), lambda: greet(Z_PEERS + [dict(dc=1)]))

    def unit_of(rows):
        wide = rows.astype(F32)
        total = jnp.sum(wide * wide, axis=-1, keepdims=True)
        return (wide * lax.rsqrt(total + 1e-06)).astype(BF16)

    for load in loads[:3]:
        load.wait()
    clu, order = clu_ref[...], ord_ref[...]
    row = iota((8, ROWS), 0)
    digits = jnp.where(
        row == 0,
        clu + 1,
        jnp.where(
            row == 1,
            order & 255,
            jnp.where(row == 2, (order >> 8) & 255, jnp.where(row == 3, order >> 16, 0)),
        ),
    ).astype(F32).astype(BF16)

    lanes = jnp.concatenate([qry_ref[...], qry_ref[...]], axis=1).astype(F32)
    column = jnp.transpose(jnp.broadcast_to(lanes, (128, 128)))[:QB]
    column = jnp.concatenate([column] * (ROWS // 128), axis=1)
    pick = jnp.where(column == iota((QB, ROWS), 1).astype(F32), 1.0, 0.0).astype(BF16)
    picked = lax.dot_general(digits, pick, (((1,), (1,)), ((), ())), preferred_element_type=F32)
    picked = meta_tile(jnp.concatenate([picked, picked], axis=1))
    lane = iota((8, 128), 1)
    for i in range(NY):
        tile = jnp.where((lane // RUN) % NY == i, picked, 0.0)
        tile = tile + pltpu.roll(tile, RUN, 1)
        qmsrc[i] = (tile + pltpu.roll(tile, 2 * RUN, 1))[0:2]
    loads[3].wait()
    qsel[...] = unit_of(jnp.dot(pick, emb_ref[...], preferred_element_type=F32))

    by_core(
        lambda: pl.semaphore_wait(barrier, len(X_PEERS) + 1),
        lambda: pl.semaphore_wait(barrier, len(Z_PEERS)),
    )

    @pl.when(c == 1)
    def _():
        pl.semaphore_signal(beside, inc=1, device_id=peer(dc=1), device_id_type=MESH)

    AT = {0: 0, -1: 1, 1: 2, -2: 3, 2: 4, -3: 5, 3: 6, 4: 7, -4: 7}

    def run_at(which):
        return pl.ds(pl.multiple_of(which * RUN, RUN), RUN)

    def block_at(at, xs, k=0, size=QB):
        return qbuf.at[pl.ds(pl.multiple_of(at * NX * QB + xs * QB + k * RUN, RUN), size)]

    sent = {"x": 0, "z": 0}

    def send(who, dx, source, target, to):
        xs = (x + dx) % NX
        n = sent[who]
        sent[who] += 1
        rcopy(block_at(source, xs), block_at(target, xs), s_g.at[n], r_g.at[target, xs], to).start()
        rcopy(qmeta.at[source, xs], qmeta.at[target, xs], s_gm.at[n], r_gm.at[target, xs], to).start()

    def along_z(who, dx, dz, step):
        send(who, dx, AT[dz], AT[dz - step], peer(dz=step))

    def along_x(dz):
        for dx in (1, 3, 2):
            send("z", 0, AT[dz], AT[dz], peer(dx=dx))

    def across(who, dx):
        t = 1 - 2 * (((x + dx) % NX) % 2)
        send(who, dx, 5 + (1 - t) // 2, 7, peer(dz=t))

    def arrive(dx, dz):
        at, xs = AT[dz], (x + dx) % NX
        rcopy(block_at(at, xs), block_at(at, xs), s_g.at[0], r_g.at[at, xs], peer(dc=1)).wait_recv()
        rcopy(qmeta.at[at, xs], qmeta.at[at, xs], s_gm.at[0], r_gm.at[at, xs], peer(dc=1)).wait_recv()

    X_RUNS = [(k, dx) for dx in (0, 1, 3, 2) for k in (2, 1, 3, 0) if (k, dx) != (0, 0)]
    Z_RUNS = [(k, dz) for dz in (0, 1, -1) for k in (2, 1, 3, 0) if (k, dz) != (0, 0)]

    def run_send(n, k, at, slot, to):
        i, back = (y + k) % NY, (NY - k) % NY
        rcopy(qsel.at[run_at(i)], block_at(at, x, back, RUN), s_q.at[n], r_q.at[slot, back], to).start()
        rcopy(qmsrc.at[i], qmrecv.at[slot, back], s_m.at[n], r_m.at[slot, back], to).start()

    def runs_arrive(at, xs, slot, own):
        for k in (0, 1, 3, 2)[own:]:
            rcopy(qsel.at[pl.ds(0, RUN)], block_at(at, xs, k, RUN), s_q.at[0], r_q.at[slot, k], peer(dc=1)).wait_recv()
            rcopy(qmsrc.at[0], qmrecv.at[slot, k], s_m.at[0], r_m.at[slot, k], peer(dc=1)).wait_recv()
        tile = qmrecv[slot, 0]
        for k in range(1, NY):
            tile = jnp.where((lane[0:2] // RUN) % NY == k, qmrecv[slot, k], tile)
        qmeta[at, xs] = tile

    def x_runs():
        for n, (k, dx) in enumerate(X_RUNS):
            run_send(n, k, 0, x, peer(dy=k, dx=dx))
        qmrecv[x, 0] = qmsrc[y]

    def z_runs():
        for n, (k, dz) in enumerate(Z_RUNS):
            run_send(n, k, AT[-dz], AT[-dz], peer(dy=k, dz=dz))
        qmrecv[0, 0] = qmsrc[y]

    by_core(x_runs, z_runs)
    block_at(0, x, 0, RUN)[...] = qsel[run_at(y)]

    unit[...] = unit_of(emb_ref[...])
    residue = clu % NY
    member = jnp.where(row == residue, 1.0, 0.0)
    before = jnp.where(iota((ROWS, ROWS), 0) < iota((ROWS, ROWS), 1), 1.0, 0.0).astype(BF16)
    prefix = jnp.dot(member.astype(BF16), before, preferred_element_type=F32)
    rank = jnp.sum(member * prefix, axis=0, keepdims=True)
    dest = residue.astype(F32) * CAP + rank
    slot_of = iota((CAP, ROWS), 0)

    def of_residue(r):
        place = jnp.where((slot_of + r * CAP).astype(F32) == dest, 1.0, 0.0).astype(BF16)
        rows = jnp.dot(place, unit[...], preferred_element_type=F32).astype(BF16)
        tile = lax.dot_general(digits, place, (((1,), (1,)), ((), ())), preferred_element_type=F32)
        return rows, meta_tile(tile)[0:2]

    PLACE = {0: 0, 1: 1, 3: 2, 2: 3}

    def key_at(j, cs):
        return kbuf.at[pl.ds(pl.multiple_of(j * 2 * CAP + cs * CAP, CAP), CAP)]

    def key_send(k):
        j, to = PLACE[k], peer(dy=k)
        rcopy(ksel.at[k], key_at(j, c), s_k.at[k], r_k.at[j, c], to).start()
        rcopy(kmsrc.at[k], kmeta.at[j, c], s_km.at[k], r_km.at[j, c], to).start()

    def key_wait(j, cs):
        rcopy(key_at(j, cs), key_at(j, cs), s_kf.at[0], r_k.at[j, cs], peer(dc=1)).wait_recv()
        rcopy(kmeta.at[j, cs], kmeta.at[j, cs], s_kmf.at[0], r_km.at[j, cs], peer(dc=1)).wait_recv()

    def key_share(j):
        rcopy(key_at(j, c), key_at(j, c), s_kf.at[j], r_k.at[j, c], peer(dc=1)).start()
        rcopy(kmeta.at[j, c], kmeta.at[j, c], s_kmf.at[j], r_km.at[j, c], peer(dc=1)).start()

    def key_codes(j):
        for cs in range(2):
            tile = kmeta[j, cs]
            code = (tile[0:1] - 1.0) * SPAN + tile[1:2]
            at = (j * 2 + cs) * CAP
            kcode[at:at + CAP, :] = jnp.transpose(jnp.broadcast_to(code, (128, CAP)))

    for k in (1, 3, 2):
        rows, tile = of_residue((y + k) % NY)
        ksel[k] = rows
        kmsrc[k] = tile
        key_send(k)
    rows, tile = of_residue(y)
    kbuf[pl.ds(pl.multiple_of(c * CAP, CAP), CAP)] = rows
    kmeta[0, c] = tile

    def x_start():
        for dx in (0, 1, 3, 2):
            xs = (x + dx) % NX
            runs_arrive(0, xs, xs, int(dx == 0))
            for step in (1, -1):
                along_z("x", dx, 0, step)

    def x_step(s):
        for dx in (0, 1, 3, 2):
            if s == 4:
                arrive(dx, 4)
                continue
            for dz in (-s, s):
                arrive(dx, dz)
                if s < 3:
                    along_z("x", dx, dz, 1 if dz < 0 else -1)
            if s == 3:
                across("x", dx)

    def z_start():
        for dz in (0, -1, 1):
            runs_arrive(AT[dz], x, AT[dz], int(dz == 0))
            if dz == 0:
                along_x(0)
            if dz != 0:
                along_z("z", 0, dz, -dz)
        for dz in (-1, 1):
            along_x(dz)

    def z_step(s):
        if s == 4:
            arrive(0, 4)
            along_x(4)
            return
        for dz in (-s, s):
            arrive(0, dz)
            if s < 3:
                along_z("z", 0, dz, 1 if dz < 0 else -1)
        if s == 3:
            across("z", 0)
        for dz in (-s, s):
            along_x(dz)

    def x_wait(s):
        for dz in ((s,) if s in (0, 4) else (-s, s)):
            for dx in (1, 3, 2):
                arrive(dx, dz)

    def rect(i0, i1, j0, j1):
        first, last = j0 * 2 * CAP, j1 * 2 * CAP
        s = lax.dot_general(
            kbuf[first:last], qbuf[i0 * NX * QB:i1 * NX * QB],
            (((1,), (1,)), ((), ())), preferred_element_type=F32,
        )
        code = kcode[first:last]
        for i in range(i0, i1):
            for p in range(2):
                tile = jnp.where(lane[0:2] < QB, qmeta[i, 2 * p], qmeta[i, 2 * p + 1])
                low = (tile[0:1] - 1.0) * SPAN
                high = low + tile[1:2]
                keep = (code >= low) & (code < high)
                at = ((i - i0) * 2 + p) * 128
                top = jnp.max(jnp.where(keep, s[:, at:at + 128], -1.0), axis=0, keepdims=True)
                best[i, p:p + 1, :] = jnp.maximum(best[i, p:p + 1, :], top)

    FAR = (0, -1, 1, -2, 2, -3, 3, 4)

    def slab_copy(i):
        return rcopy(best.at[i], zred.at[i], s_z.at[i], r_z.at[i], peer(dz=FAR[i]))

    HOME = [(k, dx) for dx in (2, 1, 3, 0) for k in (2, 1, 3, 0)]

    def home_copy(n, across):
        k, dx = HOME[n]
        if across:
            return rcopy(best.at[7], fin.at[1, y, x], s_l.at[n], r_f.at[1, y, x], peer(dy=k, dx=dx, dz=4))
        return rcopy(rtile, fin.at[0, y, x], s_f.at[n], r_f.at[0, y, x], peer(dy=k, dx=dx))

    best[...] = jnp.full(best.shape, -1.0, F32)

    def both(*steps):
        for step in steps:
            step()

    by_core(x_start, lambda: both(z_start, lambda: z_step(2), lambda: x_wait(0)))

    @pl.when(c == 0)
    def _():
        pl.semaphore_wait(beside, 1)

    key_share(0)
    key_wait(0, 1 - c)
    key_codes(0)
    rect(0, 1, 0, 1)
    by_core(lambda: x_step(1), lambda: both(lambda: z_step(3), lambda: x_wait(1)))
    rect(1, 3, 0, 1)
    for j in (1, 2):
        key_wait(j, c)
        key_share(j)
    by_core(lambda: x_step(2), lambda: both(lambda: z_step(4), lambda: x_wait(2)))
    for j in (1, 2):
        key_wait(j, 1 - c)
        key_codes(j)
    rect(0, 3, 1, 3)
    rect(3, 5, 0, 3)
    by_core(lambda: x_step(3), lambda: None)
    key_wait(3, c)
    key_share(3)
    by_core(lambda: None, lambda: x_wait(3))
    rect(5, 7, 0, 3)
    key_wait(3, 1 - c)
    key_codes(3)
    rect(0, 7, 3, 4)
    for i in range(1, 7):
        slab_copy(i).start()
    by_core(lambda: x_step(4), lambda: x_wait(4))
    rect(7, 8, 0, 4)

    for n in range(len(HOME)):
        home_copy(n, True).start()
    top = best[0]
    for i in range(1, 7):
        slab_copy(i).wait_recv()
        top = jnp.maximum(top, zred[i])
    rtile[...] = top
    for n in range(len(HOME) - 1):
        home_copy(n, False).start()
    def drain(runs, count):
        for n in range(runs):
            rcopy(qsel.at[pl.ds(0, RUN)], block_at(0, x, 0, RUN), s_q.at[n], r_q.at[0, 0], peer(dc=1)).wait_send()
            rcopy(qmsrc.at[0], qmrecv.at[0, 0], s_m.at[n], r_m.at[0, 0], peer(dc=1)).wait_send()
        for n in range(count):
            rcopy(block_at(0, x), block_at(0, x), s_g.at[n], r_g.at[0, x], peer(dc=1)).wait_send()
            rcopy(qmeta.at[0, x], qmeta.at[0, x], s_gm.at[n], r_gm.at[0, x], peer(dc=1)).wait_send()

    by_core(lambda: drain(len(X_RUNS), sent["x"]), lambda: drain(len(Z_RUNS), sent["z"]))
    for k in range(1, NY):
        rcopy(ksel.at[k], key_at(0, c), s_k.at[k], r_k.at[0, c], peer(dy=k)).wait_send()
        rcopy(kmsrc.at[k], kmeta.at[0, c], s_km.at[k], r_km.at[0, c], peer(dy=k)).wait_send()
    for j in range(NY):
        rcopy(key_at(j, c), key_at(j, c), s_kf.at[j], r_k.at[j, c], peer(dc=1)).wait_send()
        rcopy(kmeta.at[j, c], kmeta.at[j, c], s_kmf.at[j], r_km.at[j, c], peer(dc=1)).wait_send()
    for i in range(1, 7):
        slab_copy(i).wait_send()
    fin[0, y, x] = top
    for k, dx in reversed(HOME):
        ys, xs = (y + k) % NY, (x + dx) % NX
        for q in range(2):
            if q == 1 or (k, dx) != (0, 0):
                rcopy(rtile, fin.at[q, ys, xs], s_f.at[0], r_f.at[q, ys, xs], peer(dc=1)).wait_recv()
    result = jnp.zeros((8, 128), F32)
    for r in range(NY):
        tile = jnp.max(fin[:, r].reshape(2 * NX, 2, 128), axis=0)
        tile = jnp.where(x // 2 == 0, tile[0:1], tile[1:2])
        tile = jnp.broadcast_to(tile, (8, 128))
        tile = pltpu.roll(tile, (r * RUN - (x % 2) * QB - ((y - r + NY) % NY) * RUN + 256) % 128, 1)
        result = jnp.where(lane // RUN == r, tile, result)
    out_ref[...] = result[0, 0:QB]

    for n in range(len(HOME)):
        home_copy(n, True).wait_send()
        if n < len(HOME) - 1:
            home_copy(n, False).wait_send()


def body(embeddings, cluster, order, query_local):
    dma = pltpu.SemaphoreType.DMA
    out = pl.pallas_call(
        kernel,
        out_shape=jax.ShapeDtypeStruct((QB,), F32),
        in_specs=[pl.BlockSpec(memory_space=pl.ANY)] * 4,
        out_specs=pl.BlockSpec(memory_space=pltpu.VMEM),
        scratch_shapes=[
            pltpu.VMEM((ROWS, D), BF16),
            pltpu.VMEM((1, ROWS), jnp.int32),
            pltpu.VMEM((1, ROWS), jnp.int32),
            pltpu.VMEM((1, QB), jnp.int32),
            pltpu.VMEM((ROWS, D), BF16),
            pltpu.VMEM((QB, D), BF16),
            pltpu.VMEM((NY, 2, 128), F32),
            pltpu.VMEM((NX, NY, 2, 128), F32),
            pltpu.VMEM((NY, CAP, D), BF16),
            pltpu.VMEM((NY, 2, CAP), F32),
            pltpu.VMEM((NY * 2 * CAP, D), BF16),
            pltpu.VMEM((NY, 2, 2, CAP), F32),
            pltpu.VMEM((NY * 2 * CAP, 128), F32),
            pltpu.VMEM((NZ * NX * QB, D), BF16),
            pltpu.VMEM((NZ, NX, 2, 128), F32),
            pltpu.VMEM((NZ, 2, 128), F32),
            pltpu.VMEM((NZ, 2, 128), F32),
            pltpu.VMEM((2, 128), F32),
            pltpu.VMEM((2, NY, NX, 2, 128), F32),
            dma((4,)), dma((15,)), dma((15,)), dma((NX, NY)), dma((NX, NY)),
            dma((NY,)), dma((NY,)), dma((NY, 2)), dma((NY, 2)), dma((NY,)), dma((NY,)),
            dma((29,)), dma((29,)), dma((NZ, NX)), dma((NZ, NX)),
            dma((NZ,)), dma((NZ,)), dma((NY * NX,)), dma((2, NY, NX)), dma((NY * NX,)),
            pltpu.SemaphoreType.REGULAR,
        ],
        compiler_params=pltpu.CompilerParams(
            collective_id=0, has_side_effects=True, vmem_limit_bytes=54912 * 1024
        ),
        name="dedup",
    )(
        embeddings,
        cluster.reshape(1, ROWS),
        order.reshape(1, ROWS),
        query_local.reshape(1, QB),
    )
    return out


def solution(mesh):
    return jax.shard_map(
        body,
        mesh=mesh,
        in_specs=(
            P(("group", "dev"), None),
            P(("group", "dev")),
            P(("group", "dev")),
            P(("group", "dev")),
        ),
        out_specs=P(("group", "dev")),
        check_vma=False,
    )
```

```python
import jax
import jax.numpy as jnp
from jax import lax
from jax.experimental import pallas as pl
from jax.experimental.pallas import tpu as pltpu
from jax.sharding import PartitionSpec as P

MESH = pl.DeviceIdType.MESH
F32, BF16 = jnp.float32, jnp.bfloat16
NY, NX, NZ = 4, 4, 8
D = 768
ROWS = 512
QB = 64
RUN = 16
CAP = 256
SPAN = 131072.0


def iota(shape, axis):
    return lax.broadcasted_iota(jnp.int32, shape, axis)


def meta_tile(picked):
    order = picked[1:2] + 256.0 * picked[2:3] + 65536.0 * picked[3:4]
    return jnp.where(iota(picked.shape, 0) == 0, picked[0:1], order)


def kernel(
    emb_hbm, clu_hbm, ord_hbm, qry_hbm, out_ref,
    emb_ref, clu_ref, ord_ref, qry_ref,
    unit, qsel, qmsrc, qmrecv, ksel, kmsrc, kbuf, kmeta, kcode, qbuf, qmeta,
    best, zred, rtile, fin,
    s_in, s_q, s_m, r_q, r_m, s_k, s_km, r_k, r_km, s_kf, s_kmf,
    s_g, s_gm, r_g, r_gm, s_z, r_z, s_f, r_f, s_l, beside,
):
    y = lax.axis_index("group")
    d = lax.axis_index("dev")
    x, z, c = d // (2 * NZ), (d // 2) % NZ, d % 2

    loads = [
        pltpu.make_async_copy(src, dst, s_in.at[n])
        for n, (src, dst) in enumerate(
            ((qry_hbm, qry_ref), (clu_hbm, clu_ref), (ord_hbm, ord_ref), (emb_hbm, emb_ref))
        )
    ]
    for load in loads:
        load.start()

    def peer(dy=0, dx=0, dz=0, dc=0):
        return (
            (y + dy) % NY,
            (((x + dx) % NX) * NZ + (z + dz) % NZ) * 2 + (c + dc) % 2,
        )

    def rcopy(src, dst, ssem, rsem, to):
        return pltpu.make_async_remote_copy(
            src_ref=src, dst_ref=dst, send_sem=ssem, recv_sem=rsem,
            device_id=to, device_id_type=MESH,
        )

    def by_core(x_then_z, z_then_x):
        pl.when(c == 1)(x_then_z)
        pl.when(c == 0)(z_then_x)

    barrier = pltpu.get_barrier_semaphore()
    X_PEERS = [dict(dz=1), dict(dz=-1)] + [dict(dy=k // NX, dx=k % NX) for k in range(1, NY * NX)]
    Z_PEERS = [dict(dz=1), dict(dz=-1)] + [dict(dx=k) for k in range(1, NX)]
    Z_PEERS += [dict(dy=k, dz=dz) for k in range(1, NY) for dz in (0, 1, -1)]

    def greet(peers):
        for to in peers:
            pl.semaphore_signal(barrier, inc=1, device_id=peer(**to), device_id_type=MESH)

    by_core(lambda: greet(X_PEERS), lambda: greet(Z_PEERS + [dict(dc=1)]))

    def unit_of(rows):
        wide = rows.astype(F32)
        total = jnp.sum(wide * wide, axis=-1, keepdims=True)
        return (wide * lax.rsqrt(total + 1e-06)).astype(BF16)

    for load in loads[:3]:
        load.wait()
    clu, order = clu_ref[...], ord_ref[...]
    row = iota((8, ROWS), 0)
    digits = jnp.where(
        row == 0,
        clu + 1,
        jnp.where(
            row == 1,
            order & 255,
            jnp.where(row == 2, (order >> 8) & 255, jnp.where(row == 3, order >> 16, 0)),
        ),
    ).astype(F32).astype(BF16)

    lanes = jnp.concatenate([qry_ref[...], qry_ref[...]], axis=1).astype(F32)
    column = jnp.transpose(jnp.broadcast_to(lanes, (128, 128)))[:QB]
    column = jnp.concatenate([column] * (ROWS // 128), axis=1)
    pick = jnp.where(column == iota((QB, ROWS), 1).astype(F32), 1.0, 0.0).astype(BF16)
    picked = lax.dot_general(digits, pick, (((1,), (1,)), ((), ())), preferred_element_type=F32)
    picked = meta_tile(jnp.concatenate([picked, picked], axis=1))
    lane = iota((8, 128), 1)
    for i in range(NY):
        tile = jnp.where((lane // RUN) % NY == i, picked, 0.0)
        tile = tile + pltpu.roll(tile, RUN, 1)
        qmsrc[i] = (tile + pltpu.roll(tile, 2 * RUN, 1))[0:2]
    loads[3].wait()
    qsel[...] = unit_of(jnp.dot(pick, emb_ref[...], preferred_element_type=F32))

    by_core(
        lambda: pl.semaphore_wait(barrier, len(X_PEERS) + 1),
        lambda: pl.semaphore_wait(barrier, len(Z_PEERS)),
    )

    @pl.when(c == 1)
    def _():
        pl.semaphore_signal(beside, inc=1, device_id=peer(dc=1), device_id_type=MESH)

    AT = {0: 0, -1: 1, 1: 2, -2: 3, 2: 4, -3: 5, 3: 6, 4: 7, -4: 7}

    def run_at(which):
        return pl.ds(pl.multiple_of(which * RUN, RUN), RUN)

    def block_at(at, xs, k=0, size=QB):
        return qbuf.at[pl.ds(pl.multiple_of(at * NX * QB + xs * QB + k * RUN, RUN), size)]

    sent = {"x": 0, "z": 0}

    def send(who, dx, source, target, to):
        xs = (x + dx) % NX
        n = sent[who]
        sent[who] += 1
        rcopy(block_at(source, xs), block_at(target, xs), s_g.at[n], r_g.at[target, xs], to).start()
        rcopy(qmeta.at[source, xs], qmeta.at[target, xs], s_gm.at[n], r_gm.at[target, xs], to).start()

    def along_z(who, dx, dz, step):
        send(who, dx, AT[dz], AT[dz - step], peer(dz=step))

    def along_x(dz):
        for dx in (2, 1, 3):
            send("z", 0, AT[dz], AT[dz], peer(dx=dx))

    def across(who, dx):
        t = 1 - 2 * (((x + dx) % NX) % 2)
        send(who, dx, 5 + (1 - t) // 2, 7, peer(dz=t))

    def arrive(dx, dz):
        at, xs = AT[dz], (x + dx) % NX
        rcopy(block_at(at, xs), block_at(at, xs), s_g.at[0], r_g.at[at, xs], peer(dc=1)).wait_recv()
        rcopy(qmeta.at[at, xs], qmeta.at[at, xs], s_gm.at[0], r_gm.at[at, xs], peer(dc=1)).wait_recv()

    X_RUNS = [(k, dx) for dx in (0, 1, 3, 2) for k in (2, 1, 3, 0) if (k, dx) != (0, 0)]
    Z_RUNS = [(k, dz) for dz in (0, 1, -1) for k in (2, 1, 3, 0) if (k, dz) != (0, 0)]

    def run_send(n, k, at, slot, to):
        i, back = (y + k) % NY, (NY - k) % NY
        rcopy(qsel.at[run_at(i)], block_at(at, x, back, RUN), s_q.at[n], r_q.at[slot, back], to).start()
        rcopy(qmsrc.at[i], qmrecv.at[slot, back], s_m.at[n], r_m.at[slot, back], to).start()

    def runs_arrive(at, xs, slot, own):
        for k in (0, 1, 3, 2)[own:]:
            rcopy(qsel.at[pl.ds(0, RUN)], block_at(at, xs, k, RUN), s_q.at[0], r_q.at[slot, k], peer(dc=1)).wait_recv()
            rcopy(qmsrc.at[0], qmrecv.at[slot, k], s_m.at[0], r_m.at[slot, k], peer(dc=1)).wait_recv()
        tile = qmrecv[slot, 0]
        for k in range(1, NY):
            tile = jnp.where((lane[0:2] // RUN) % NY == k, qmrecv[slot, k], tile)
        qmeta[at, xs] = tile

    def x_runs():
        for n, (k, dx) in enumerate(X_RUNS):
            run_send(n, k, 0, x, peer(dy=k, dx=dx))
        qmrecv[x, 0] = qmsrc[y]

    def z_runs():
        for n, (k, dz) in enumerate(Z_RUNS):
            run_send(n, k, AT[-dz], AT[-dz], peer(dy=k, dz=dz))
        qmrecv[0, 0] = qmsrc[y]

    by_core(x_runs, z_runs)
    block_at(0, x, 0, RUN)[...] = qsel[run_at(y)]

    unit[...] = unit_of(emb_ref[...])
    residue = clu % NY
    member = jnp.where(row == residue, 1.0, 0.0)
    before = jnp.where(iota((ROWS, ROWS), 0) < iota((ROWS, ROWS), 1), 1.0, 0.0).astype(BF16)
    prefix = jnp.dot(member.astype(BF16), before, preferred_element_type=F32)
    rank = jnp.sum(member * prefix, axis=0, keepdims=True)
    dest = residue.astype(F32) * CAP + rank
    slot_of = iota((CAP, ROWS), 0)

    def of_residue(r):
        place = jnp.where((slot_of + r * CAP).astype(F32) == dest, 1.0, 0.0).astype(BF16)
        rows = jnp.dot(place, unit[...], preferred_element_type=F32).astype(BF16)
        tile = lax.dot_general(digits, place, (((1,), (1,)), ((), ())), preferred_element_type=F32)
        return rows, meta_tile(tile)[0:2]

    PLACE = {0: 0, 1: 1, 3: 2, 2: 3}

    def key_at(j, cs):
        return kbuf.at[pl.ds(pl.multiple_of(j * 2 * CAP + cs * CAP, CAP), CAP)]

    def key_send(k):
        j, to = PLACE[k], peer(dy=k)
        rcopy(ksel.at[k], key_at(j, c), s_k.at[k], r_k.at[j, c], to).start()
        rcopy(kmsrc.at[k], kmeta.at[j, c], s_km.at[k], r_km.at[j, c], to).start()

    def key_wait(j, cs):
        rcopy(key_at(j, cs), key_at(j, cs), s_kf.at[0], r_k.at[j, cs], peer(dc=1)).wait_recv()
        rcopy(kmeta.at[j, cs], kmeta.at[j, cs], s_kmf.at[0], r_km.at[j, cs], peer(dc=1)).wait_recv()

    def key_share(j):
        rcopy(key_at(j, c), key_at(j, c), s_kf.at[j], r_k.at[j, c], peer(dc=1)).start()
        rcopy(kmeta.at[j, c], kmeta.at[j, c], s_kmf.at[j], r_km.at[j, c], peer(dc=1)).start()

    def key_codes(j):
        for cs in range(2):
            tile = kmeta[j, cs]
            code = (tile[0:1] - 1.0) * SPAN + tile[1:2]
            at = (j * 2 + cs) * CAP
            kcode[at:at + CAP, :] = jnp.transpose(jnp.broadcast_to(code, (128, CAP)))

    for k in (1, 3, 2):
        rows, tile = of_residue((y + k) % NY)
        ksel[k] = rows
        kmsrc[k] = tile
        key_send(k)
    rows, tile = of_residue(y)
    kbuf[pl.ds(pl.multiple_of(c * CAP, CAP), CAP)] = rows
    kmeta[0, c] = tile

    def x_start():
        for dx in (0, 1, 3, 2):
            xs = (x + dx) % NX
            runs_arrive(0, xs, xs, int(dx == 0))
            for step in (1, -1):
                along_z("x", dx, 0, step)

    def x_step(s):
        for dx in (0, 1, 3, 2):
            if s == 4:
                arrive(dx, 4)
                continue
            for dz in (-s, s):
                arrive(dx, dz)
                if s < 3:
                    along_z("x", dx, dz, 1 if dz < 0 else -1)
            if s == 3:
                across("x", dx)

    def z_start():
        for dz in (0, -1, 1):
            runs_arrive(AT[dz], x, AT[dz], int(dz == 0))
            if dz == 0:
                along_x(0)
            if dz != 0:
                along_z("z", 0, dz, -dz)
        for dz in (-1, 1):
            along_x(dz)

    def z_step(s):
        if s == 4:
            arrive(0, 4)
            along_x(4)
            return
        for dz in (-s, s):
            arrive(0, dz)
            if s < 3:
                along_z("z", 0, dz, 1 if dz < 0 else -1)
        if s == 3:
            across("z", 0)
        for dz in (-s, s):
            along_x(dz)

    def x_wait(s):
        for dz in ((s,) if s in (0, 4) else (-s, s)):
            for dx in (1, 3, 2):
                arrive(dx, dz)

    def rect(i0, i1, j0, j1):
        first, last = j0 * 2 * CAP, j1 * 2 * CAP
        s = lax.dot_general(
            kbuf[first:last], qbuf[i0 * NX * QB:i1 * NX * QB],
            (((1,), (1,)), ((), ())), preferred_element_type=F32,
        )
        code = kcode[first:last]
        for i in range(i0, i1):
            for p in range(2):
                tile = jnp.where(lane[0:2] < QB, qmeta[i, 2 * p], qmeta[i, 2 * p + 1])
                low = (tile[0:1] - 1.0) * SPAN
                high = low + tile[1:2]
                keep = (code >= low) & (code < high)
                at = ((i - i0) * 2 + p) * 128
                top = jnp.max(jnp.where(keep, s[:, at:at + 128], -1.0), axis=0, keepdims=True)
                best[i, p:p + 1, :] = jnp.maximum(best[i, p:p + 1, :], top)

    FAR = (0, -1, 1, -2, 2, -3, 3, 4)

    def slab_copy(i):
        return rcopy(best.at[i], zred.at[i], s_z.at[i], r_z.at[i], peer(dz=FAR[i]))

    HOME = [(k, dx) for dx in (2, 1, 3, 0) for k in (2, 1, 3, 0)]

    def home_copy(n, across):
        k, dx = HOME[n]
        if across:
            return rcopy(best.at[7], fin.at[1, y, x], s_l.at[n], r_f.at[1, y, x], peer(dy=k, dx=dx, dz=4))
        return rcopy(rtile, fin.at[0, y, x], s_f.at[n], r_f.at[0, y, x], peer(dy=k, dx=dx))

    best[...] = jnp.full(best.shape, -1.0, F32)

    def both(*steps):
        for step in steps:
            step()

    by_core(x_start, lambda: both(z_start, lambda: z_step(2), lambda: x_wait(0)))

    @pl.when(c == 0)
    def _():
        pl.semaphore_wait(beside, 1)

    key_share(0)
    key_wait(0, 1 - c)
    key_codes(0)
    rect(0, 1, 0, 1)
    by_core(lambda: x_step(1), lambda: both(lambda: z_step(3), lambda: x_wait(1)))
    rect(1, 3, 0, 1)
    for j in (1, 2):
        key_wait(j, c)
        key_share(j)
    by_core(lambda: x_step(2), lambda: both(lambda: z_step(4), lambda: x_wait(2)))
    for j in (1, 2):
        key_wait(j, 1 - c)
        key_codes(j)
    rect(0, 3, 1, 3)
    rect(3, 5, 0, 3)
    by_core(lambda: x_step(3), lambda: None)
    key_wait(3, c)
    key_share(3)
    by_core(lambda: None, lambda: x_wait(3))
    rect(5, 7, 0, 3)
    key_wait(3, 1 - c)
    key_codes(3)
    rect(0, 7, 3, 4)
    for i in range(1, 7):
        slab_copy(i).start()
    by_core(lambda: x_step(4), lambda: x_wait(4))
    rect(7, 8, 0, 4)

    for n in range(len(HOME)):
        home_copy(n, True).start()
    top = best[0]
    for i in range(1, 7):
        slab_copy(i).wait_recv()
        top = jnp.maximum(top, zred[i])
    rtile[...] = top
    for n in range(len(HOME) - 1):
        home_copy(n, False).start()
    def drain(runs, count):
        for n in range(runs):
            rcopy(qsel.at[pl.ds(0, RUN)], block_at(0, x, 0, RUN), s_q.at[n], r_q.at[0, 0], peer(dc=1)).wait_send()
            rcopy(qmsrc.at[0], qmrecv.at[0, 0], s_m.at[n], r_m.at[0, 0], peer(dc=1)).wait_send()
        for n in range(count):
            rcopy(block_at(0, x), block_at(0, x), s_g.at[n], r_g.at[0, x], peer(dc=1)).wait_send()
            rcopy(qmeta.at[0, x], qmeta.at[0, x], s_gm.at[n], r_gm.at[0, x], peer(dc=1)).wait_send()

    by_core(lambda: drain(len(X_RUNS), sent["x"]), lambda: drain(len(Z_RUNS), sent["z"]))
    for k in range(1, NY):
        rcopy(ksel.at[k], key_at(0, c), s_k.at[k], r_k.at[0, c], peer(dy=k)).wait_send()
        rcopy(kmsrc.at[k], kmeta.at[0, c], s_km.at[k], r_km.at[0, c], peer(dy=k)).wait_send()
    for j in range(NY):
        rcopy(key_at(j, c), key_at(j, c), s_kf.at[j], r_k.at[j, c], peer(dc=1)).wait_send()
        rcopy(kmeta.at[j, c], kmeta.at[j, c], s_kmf.at[j], r_km.at[j, c], peer(dc=1)).wait_send()
    for i in range(1, 7):
        slab_copy(i).wait_send()
    fin[0, y, x] = top
    for k, dx in reversed(HOME):
        ys, xs = (y + k) % NY, (x + dx) % NX
        for q in range(2):
            if q == 1 or (k, dx) != (0, 0):
                rcopy(rtile, fin.at[q, ys, xs], s_f.at[0], r_f.at[q, ys, xs], peer(dc=1)).wait_recv()
    result = jnp.zeros((8, 128), F32)
    for r in range(NY):
        tile = jnp.max(fin[:, r].reshape(2 * NX, 2, 128), axis=0)
        tile = jnp.where(x // 2 == 0, tile[0:1], tile[1:2])
        tile = jnp.broadcast_to(tile, (8, 128))
        tile = pltpu.roll(tile, (r * RUN - (x % 2) * QB - ((y - r + NY) % NY) * RUN + 256) % 128, 1)
        result = jnp.where(lane // RUN == r, tile, result)
    out_ref[...] = result[0, 0:QB]

    for n in range(len(HOME)):
        home_copy(n, True).wait_send()
        if n < len(HOME) - 1:
            home_copy(n, False).wait_send()


def body(embeddings, cluster, order, query_local):
    dma = pltpu.SemaphoreType.DMA
    out = pl.pallas_call(
        kernel,
        out_shape=jax.ShapeDtypeStruct((QB,), F32),
        in_specs=[pl.BlockSpec(memory_space=pl.ANY)] * 4,
        out_specs=pl.BlockSpec(memory_space=pltpu.VMEM),
        scratch_shapes=[
            pltpu.VMEM((ROWS, D), BF16),
            pltpu.VMEM((1, ROWS), jnp.int32),
            pltpu.VMEM((1, ROWS), jnp.int32),
            pltpu.VMEM((1, QB), jnp.int32),
            pltpu.VMEM((ROWS, D), BF16),
            pltpu.VMEM((QB, D), BF16),
            pltpu.VMEM((NY, 2, 128), F32),
            pltpu.VMEM((NX, NY, 2, 128), F32),
            pltpu.VMEM((NY, CAP, D), BF16),
            pltpu.VMEM((NY, 2, CAP), F32),
            pltpu.VMEM((NY * 2 * CAP, D), BF16),
            pltpu.VMEM((NY, 2, 2, CAP), F32),
            pltpu.VMEM((NY * 2 * CAP, 128), F32),
            pltpu.VMEM((NZ * NX * QB, D), BF16),
            pltpu.VMEM((NZ, NX, 2, 128), F32),
            pltpu.VMEM((NZ, 2, 128), F32),
            pltpu.VMEM((NZ, 2, 128), F32),
            pltpu.VMEM((2, 128), F32),
            pltpu.VMEM((2, NY, NX, 2, 128), F32),
            dma((4,)), dma((15,)), dma((15,)), dma((NX, NY)), dma((NX, NY)),
            dma((NY,)), dma((NY,)), dma((NY, 2)), dma((NY, 2)), dma((NY,)), dma((NY,)),
            dma((29,)), dma((29,)), dma((NZ, NX)), dma((NZ, NX)),
            dma((NZ,)), dma((NZ,)), dma((NY * NX,)), dma((2, NY, NX)), dma((NY * NX,)),
            pltpu.SemaphoreType.REGULAR,
        ],
        compiler_params=pltpu.CompilerParams(
            collective_id=0, has_side_effects=True, vmem_limit_bytes=54912 * 1024
        ),
        name="dedup",
    )(
        embeddings,
        cluster.reshape(1, ROWS),
        order.reshape(1, ROWS),
        query_local.reshape(1, QB),
    )
    return out


def solution(mesh):
    return jax.shard_map(
        body,
        mesh=mesh,
        in_specs=(
            P(("group", "dev"), None),
            P(("group", "dev")),
            P(("group", "dev")),
            P(("group", "dev")),
        ),
        out_specs=P(("group", "dev")),
        check_vma=False,
    )
```

```python
import jax
import jax.numpy as jnp
from jax import lax
from jax.experimental import pallas as pl
from jax.experimental.pallas import tpu as pltpu
from jax.sharding import PartitionSpec as P

MESH = pl.DeviceIdType.MESH
F32, BF16 = jnp.float32, jnp.bfloat16
NY, NX, NZ = 4, 4, 8
D = 768
ROWS = 512
QB = 64
RUN = 16
CAP = 256
SPAN = 131072.0


def iota(shape, axis):
    return lax.broadcasted_iota(jnp.int32, shape, axis)


def meta_tile(picked):
    order = picked[1:2] + 256.0 * picked[2:3] + 65536.0 * picked[3:4]
    return jnp.where(iota(picked.shape, 0) == 0, picked[0:1], order)


def kernel(
    emb_hbm, clu_hbm, ord_hbm, qry_hbm, out_ref,
    emb_ref, clu_ref, ord_ref, qry_ref,
    unit, qsel, qmsrc, qmrecv, ksel, kmsrc, kbuf, kmeta, kcode, qbuf, qmeta,
    best, zred, rtile, fin,
    s_in, s_q, s_m, r_q, r_m, s_k, s_km, r_k, r_km, s_kf, s_kmf,
    s_g, s_gm, r_g, r_gm, s_z, r_z, s_f, r_f, s_l, beside,
):
    y = lax.axis_index("group")
    d = lax.axis_index("dev")
    x, z, c = d // (2 * NZ), (d // 2) % NZ, d % 2

    loads = [
        pltpu.make_async_copy(src, dst, s_in.at[n])
        for n, (src, dst) in enumerate(
            ((qry_hbm, qry_ref), (clu_hbm, clu_ref), (ord_hbm, ord_ref), (emb_hbm, emb_ref))
        )
    ]
    for load in loads:
        load.start()

    def peer(dy=0, dx=0, dz=0, dc=0):
        return (
            (y + dy) % NY,
            (((x + dx) % NX) * NZ + (z + dz) % NZ) * 2 + (c + dc) % 2,
        )

    def rcopy(src, dst, ssem, rsem, to):
        return pltpu.make_async_remote_copy(
            src_ref=src, dst_ref=dst, send_sem=ssem, recv_sem=rsem,
            device_id=to, device_id_type=MESH,
        )

    def by_core(x_then_z, z_then_x):
        pl.when(c == 1)(x_then_z)
        pl.when(c == 0)(z_then_x)

    barrier = pltpu.get_barrier_semaphore()
    X_PEERS = [dict(dz=1), dict(dz=-1)] + [dict(dy=k // NX, dx=k % NX) for k in range(1, NY * NX)]
    Z_PEERS = [dict(dz=1), dict(dz=-1)] + [dict(dx=k) for k in range(1, NX)]
    Z_PEERS += [dict(dy=k, dz=dz) for k in range(1, NY) for dz in (0, 1, -1)]

    def greet(peers):
        for to in peers:
            pl.semaphore_signal(barrier, inc=1, device_id=peer(**to), device_id_type=MESH)

    by_core(lambda: greet(X_PEERS), lambda: greet(Z_PEERS + [dict(dc=1)]))

    def unit_of(rows):
        wide = rows.astype(F32)
        total = jnp.sum(wide * wide, axis=-1, keepdims=True)
        return (wide * lax.rsqrt(total + 1e-06)).astype(BF16)

    for load in loads[:3]:
        load.wait()
    clu, order = clu_ref[...], ord_ref[...]
    row = iota((8, ROWS), 0)
    digits = jnp.where(
        row == 0,
        clu + 1,
        jnp.where(
            row == 1,
            order & 255,
            jnp.where(row == 2, (order >> 8) & 255, jnp.where(row == 3, order >> 16, 0)),
        ),
    ).astype(F32).astype(BF16)

    lanes = jnp.concatenate([qry_ref[...], qry_ref[...]], axis=1).astype(F32)
    column = jnp.transpose(jnp.broadcast_to(lanes, (128, 128)))[:QB]
    column = jnp.concatenate([column] * (ROWS // 128), axis=1)
    pick = jnp.where(column == iota((QB, ROWS), 1).astype(F32), 1.0, 0.0).astype(BF16)
    picked = lax.dot_general(digits, pick, (((1,), (1,)), ((), ())), preferred_element_type=F32)
    picked = meta_tile(jnp.concatenate([picked, picked], axis=1))
    lane = iota((8, 128), 1)
    for i in range(NY):
        tile = jnp.where((lane // RUN) % NY == i, picked, 0.0)
        tile = tile + pltpu.roll(tile, RUN, 1)
        qmsrc[i] = (tile + pltpu.roll(tile, 2 * RUN, 1))[0:2]
    loads[3].wait()
    qsel[...] = unit_of(jnp.dot(pick, emb_ref[...], preferred_element_type=F32))

    by_core(
        lambda: pl.semaphore_wait(barrier, len(X_PEERS) + 1),
        lambda: pl.semaphore_wait(barrier, len(Z_PEERS)),
    )

    @pl.when(c == 1)
    def _():
        pl.semaphore_signal(beside, inc=1, device_id=peer(dc=1), device_id_type=MESH)

    AT = {0: 0, -1: 1, 1: 2, -2: 3, 2: 4, -3: 5, 3: 6, 4: 7, -4: 7}

    def run_at(which):
        return pl.ds(pl.multiple_of(which * RUN, RUN), RUN)

    def block_at(at, xs, k=0, size=QB):
        return qbuf.at[pl.ds(pl.multiple_of(at * NX * QB + xs * QB + k * RUN, RUN), size)]

    sent = {"x": 0, "z": 0}

    def send(who, dx, source, target, to):
        xs = (x + dx) % NX
        n = sent[who]
        sent[who] += 1
        rcopy(block_at(source, xs), block_at(target, xs), s_g.at[n], r_g.at[target, xs], to).start()
        rcopy(qmeta.at[source, xs], qmeta.at[target, xs], s_gm.at[n], r_gm.at[target, xs], to).start()

    def along_z(who, dx, dz, step):
        send(who, dx, AT[dz], AT[dz - step], peer(dz=step))

    def along_x(dz):
        for dx in (2, 1, 3):
            send("z", 0, AT[dz], AT[dz], peer(dx=dx))

    def across(who, dx):
        t = 1 - 2 * (((x + dx) % NX) % 2)
        send(who, dx, 5 + (1 - t) // 2, 7, peer(dz=t))

    def arrive(dx, dz):
        at, xs = AT[dz], (x + dx) % NX
        rcopy(block_at(at, xs), block_at(at, xs), s_g.at[0], r_g.at[at, xs], peer(dc=1)).wait_recv()
        rcopy(qmeta.at[at, xs], qmeta.at[at, xs], s_gm.at[0], r_gm.at[at, xs], peer(dc=1)).wait_recv()

    X_RUNS = [(k, dx) for dx in (0, 1, 3, 2) for k in (2, 1, 3, 0) if (k, dx) != (0, 0)]
    Z_RUNS = [(k, dz) for dz in (0, 1, -1) for k in (2, 1, 3, 0) if (k, dz) != (0, 0)]

    def run_send(n, k, at, slot, to):
        i, back = (y + k) % NY, (NY - k) % NY
        rcopy(qsel.at[run_at(i)], block_at(at, x, back, RUN), s_q.at[n], r_q.at[slot, back], to).start()
        rcopy(qmsrc.at[i], qmrecv.at[slot, back], s_m.at[n], r_m.at[slot, back], to).start()

    def runs_arrive(at, xs, slot, own):
        for k in (0, 1, 3, 2)[own:]:
            rcopy(qsel.at[pl.ds(0, RUN)], block_at(at, xs, k, RUN), s_q.at[0], r_q.at[slot, k], peer(dc=1)).wait_recv()
            rcopy(qmsrc.at[0], qmrecv.at[slot, k], s_m.at[0], r_m.at[slot, k], peer(dc=1)).wait_recv()
        tile = qmrecv[slot, 0]
        for k in range(1, NY):
            tile = jnp.where((lane[0:2] // RUN) % NY == k, qmrecv[slot, k], tile)
        qmeta[at, xs] = tile

    def x_runs():
        for n, (k, dx) in enumerate(X_RUNS):
            run_send(n, k, 0, x, peer(dy=k, dx=dx))
        qmrecv[x, 0] = qmsrc[y]

    def z_runs():
        for n, (k, dz) in enumerate(Z_RUNS):
            run_send(n, k, AT[-dz], AT[-dz], peer(dy=k, dz=dz))
        qmrecv[0, 0] = qmsrc[y]

    by_core(x_runs, z_runs)
    block_at(0, x, 0, RUN)[...] = qsel[run_at(y)]

    unit[...] = unit_of(emb_ref[...])
    residue = clu % NY
    member = jnp.where(row == residue, 1.0, 0.0)
    before = jnp.where(iota((ROWS, ROWS), 0) < iota((ROWS, ROWS), 1), 1.0, 0.0).astype(BF16)
    prefix = jnp.dot(member.astype(BF16), before, preferred_element_type=F32)
    rank = jnp.sum(member * prefix, axis=0, keepdims=True)
    dest = residue.astype(F32) * CAP + rank
    slot_of = iota((CAP, ROWS), 0)

    def of_residue(r):
        place = jnp.where((slot_of + r * CAP).astype(F32) == dest, 1.0, 0.0).astype(BF16)
        rows = jnp.dot(place, unit[...], preferred_element_type=F32).astype(BF16)
        tile = lax.dot_general(digits, place, (((1,), (1,)), ((), ())), preferred_element_type=F32)
        return rows, meta_tile(tile)[0:2]

    PLACE = {0: 0, 1: 1, 3: 2, 2: 3}

    def key_at(j, cs):
        return kbuf.at[pl.ds(pl.multiple_of(j * 2 * CAP + cs * CAP, CAP), CAP)]

    def key_send(k):
        j, to = PLACE[k], peer(dy=k)
        rcopy(ksel.at[k], key_at(j, c), s_k.at[k], r_k.at[j, c], to).start()
        rcopy(kmsrc.at[k], kmeta.at[j, c], s_km.at[k], r_km.at[j, c], to).start()

    def key_wait(j, cs):
        rcopy(key_at(j, cs), key_at(j, cs), s_kf.at[0], r_k.at[j, cs], peer(dc=1)).wait_recv()
        rcopy(kmeta.at[j, cs], kmeta.at[j, cs], s_kmf.at[0], r_km.at[j, cs], peer(dc=1)).wait_recv()

    def key_share(j):
        rcopy(key_at(j, c), key_at(j, c), s_kf.at[j], r_k.at[j, c], peer(dc=1)).start()
        rcopy(kmeta.at[j, c], kmeta.at[j, c], s_kmf.at[j], r_km.at[j, c], peer(dc=1)).start()

    def key_codes(j):
        for cs in range(2):
            tile = kmeta[j, cs]
            code = (tile[0:1] - 1.0) * SPAN + tile[1:2]
            at = (j * 2 + cs) * CAP
            kcode[at:at + CAP, :] = jnp.transpose(jnp.broadcast_to(code, (128, CAP)))

    def key_begin(k):
        rows, tile = of_residue((y + k) % NY)
        ksel[k] = rows
        kmsrc[k] = tile
        key_send(k)

    key_begin(1)
    key_begin(3)
    rows, tile = of_residue(y)
    kbuf[pl.ds(pl.multiple_of(c * CAP, CAP), CAP)] = rows
    kmeta[0, c] = tile
    key_begin(2)

    def x_start():
        for dx in (0, 1, 3, 2):
            xs = (x + dx) % NX
            runs_arrive(0, xs, xs, int(dx == 0))
            for step in (1, -1):
                along_z("x", dx, 0, step)

    def x_step(s):
        for dx in (0, 1, 3, 2):
            if s == 4:
                arrive(dx, 4)
                continue
            for dz in (-s, s):
                arrive(dx, dz)
                if s < 3:
                    along_z("x", dx, dz, 1 if dz < 0 else -1)
            if s == 3:
                across("x", dx)

    def z_start():
        for dz in (0, -1, 1):
            runs_arrive(AT[dz], x, AT[dz], int(dz == 0))
            if dz == 0:
                along_x(0)
            if dz != 0:
                along_z("z", 0, dz, -dz)
        for dz in (-1, 1):
            along_x(dz)

    def z_step(s):
        if s == 4:
            arrive(0, 4)
            along_x(4)
            return
        for dz in (-s, s):
            arrive(0, dz)
            if s < 3:
                along_z("z", 0, dz, 1 if dz < 0 else -1)
        if s == 3:
            across("z", 0)
        for dz in (-s, s):
            along_x(dz)

    def x_wait(s):
        for dz in ((s,) if s in (0, 4) else (-s, s)):
            for dx in (1, 3, 2):
                arrive(dx, dz)

    def rect(i0, i1, j0, j1):
        first, last = j0 * 2 * CAP, j1 * 2 * CAP
        s = lax.dot_general(
            kbuf[first:last], qbuf[i0 * NX * QB:i1 * NX * QB],
            (((1,), (1,)), ((), ())), preferred_element_type=F32,
        )
        code = kcode[first:last]
        for i in range(i0, i1):
            for p in range(2):
                tile = jnp.where(lane[0:2] < QB, qmeta[i, 2 * p], qmeta[i, 2 * p + 1])
                low = (tile[0:1] - 1.0) * SPAN
                high = low + tile[1:2]
                keep = (code >= low) & (code < high)
                at = ((i - i0) * 2 + p) * 128
                top = jnp.max(jnp.where(keep, s[:, at:at + 128], -1.0), axis=0, keepdims=True)
                best[i, p:p + 1, :] = jnp.maximum(best[i, p:p + 1, :], top)

    FAR = (0, -1, 1, -2, 2, -3, 3, 4)

    def slab_copy(i):
        return rcopy(best.at[i], zred.at[i], s_z.at[i], r_z.at[i], peer(dz=FAR[i]))

    HOME = [(k, dx) for dx in (2, 1, 3, 0) for k in (2, 1, 3, 0)]

    def home_copy(n, across):
        k, dx = HOME[n]
        if across:
            return rcopy(best.at[7], fin.at[1, y, x], s_l.at[n], r_f.at[1, y, x], peer(dy=k, dx=dx, dz=4))
        return rcopy(rtile, fin.at[0, y, x], s_f.at[n], r_f.at[0, y, x], peer(dy=k, dx=dx))

    best[...] = jnp.full(best.shape, -1.0, F32)

    def both(*steps):
        for step in steps:
            step()

    by_core(x_start, lambda: both(z_start, lambda: z_step(2), lambda: x_wait(0)))

    @pl.when(c == 0)
    def _():
        pl.semaphore_wait(beside, 1)

    key_share(0)
    key_wait(0, 1 - c)
    key_codes(0)
    rect(0, 1, 0, 1)
    by_core(lambda: x_step(1), lambda: both(lambda: z_step(3), lambda: x_wait(1)))
    rect(1, 3, 0, 1)
    for j in (1, 2):
        key_wait(j, c)
        key_share(j)
    by_core(lambda: x_step(2), lambda: both(lambda: z_step(4), lambda: x_wait(2)))
    for j in (1, 2):
        key_wait(j, 1 - c)
        key_codes(j)
    rect(0, 3, 1, 3)
    rect(3, 5, 0, 3)
    by_core(lambda: x_step(3), lambda: None)
    key_wait(3, c)
    key_share(3)
    by_core(lambda: None, lambda: x_wait(3))
    rect(5, 7, 0, 3)
    key_wait(3, 1 - c)
    key_codes(3)
    rect(0, 7, 3, 4)
    for i in range(1, 7):
        slab_copy(i).start()
    by_core(lambda: x_step(4), lambda: x_wait(4))
    rect(7, 8, 0, 4)

    for n in range(len(HOME)):
        home_copy(n, True).start()
    top = best[0]
    for i in range(1, 7):
        slab_copy(i).wait_recv()
        top = jnp.maximum(top, zred[i])
    rtile[...] = top
    for n in range(len(HOME) - 1):
        home_copy(n, False).start()
    def drain(runs, count):
        for n in range(runs):
            rcopy(qsel.at[pl.ds(0, RUN)], block_at(0, x, 0, RUN), s_q.at[n], r_q.at[0, 0], peer(dc=1)).wait_send()
            rcopy(qmsrc.at[0], qmrecv.at[0, 0], s_m.at[n], r_m.at[0, 0], peer(dc=1)).wait_send()
        for n in range(count):
            rcopy(block_at(0, x), block_at(0, x), s_g.at[n], r_g.at[0, x], peer(dc=1)).wait_send()
            rcopy(qmeta.at[0, x], qmeta.at[0, x], s_gm.at[n], r_gm.at[0, x], peer(dc=1)).wait_send()

    by_core(lambda: drain(len(X_RUNS), sent["x"]), lambda: drain(len(Z_RUNS), sent["z"]))
    for k in range(1, NY):
        rcopy(ksel.at[k], key_at(0, c), s_k.at[k], r_k.at[0, c], peer(dy=k)).wait_send()
        rcopy(kmsrc.at[k], kmeta.at[0, c], s_km.at[k], r_km.at[0, c], peer(dy=k)).wait_send()
    for j in range(NY):
        rcopy(key_at(j, c), key_at(j, c), s_kf.at[j], r_k.at[j, c], peer(dc=1)).wait_send()
        rcopy(kmeta.at[j, c], kmeta.at[j, c], s_kmf.at[j], r_km.at[j, c], peer(dc=1)).wait_send()
    for i in range(1, 7):
        slab_copy(i).wait_send()
    fin[0, y, x] = top
    for k, dx in reversed(HOME):
        ys, xs = (y + k) % NY, (x + dx) % NX
        for q in range(2):
            if q == 1 or (k, dx) != (0, 0):
                rcopy(rtile, fin.at[q, ys, xs], s_f.at[0], r_f.at[q, ys, xs], peer(dc=1)).wait_recv()
    result = jnp.zeros((8, 128), F32)
    for r in range(NY):
        tile = jnp.max(fin[:, r].reshape(2 * NX, 2, 128), axis=0)
        tile = jnp.where(x // 2 == 0, tile[0:1], tile[1:2])
        tile = jnp.broadcast_to(tile, (8, 128))
        tile = pltpu.roll(tile, (r * RUN - (x % 2) * QB - ((y - r + NY) % NY) * RUN + 256) % 128, 1)
        result = jnp.where(lane // RUN == r, tile, result)
    out_ref[...] = result[0, 0:QB]

    for n in range(len(HOME)):
        home_copy(n, True).wait_send()
        if n < len(HOME) - 1:
            home_copy(n, False).wait_send()


def body(embeddings, cluster, order, query_local):
    dma = pltpu.SemaphoreType.DMA
    out = pl.pallas_call(
        kernel,
        out_shape=jax.ShapeDtypeStruct((QB,), F32),
        in_specs=[pl.BlockSpec(memory_space=pl.ANY)] * 4,
        out_specs=pl.BlockSpec(memory_space=pltpu.VMEM),
        scratch_shapes=[
            pltpu.VMEM((ROWS, D), BF16),
            pltpu.VMEM((1, ROWS), jnp.int32),
            pltpu.VMEM((1, ROWS), jnp.int32),
            pltpu.VMEM((1, QB), jnp.int32),
            pltpu.VMEM((ROWS, D), BF16),
            pltpu.VMEM((QB, D), BF16),
            pltpu.VMEM((NY, 2, 128), F32),
            pltpu.VMEM((NX, NY, 2, 128), F32),
            pltpu.VMEM((NY, CAP, D), BF16),
            pltpu.VMEM((NY, 2, CAP), F32),
            pltpu.VMEM((NY * 2 * CAP, D), BF16),
            pltpu.VMEM((NY, 2, 2, CAP), F32),
            pltpu.VMEM((NY * 2 * CAP, 128), F32),
            pltpu.VMEM((NZ * NX * QB, D), BF16),
            pltpu.VMEM((NZ, NX, 2, 128), F32),
            pltpu.VMEM((NZ, 2, 128), F32),
            pltpu.VMEM((NZ, 2, 128), F32),
            pltpu.VMEM((2, 128), F32),
            pltpu.VMEM((2, NY, NX, 2, 128), F32),
            dma((4,)), dma((15,)), dma((15,)), dma((NX, NY)), dma((NX, NY)),
            dma((NY,)), dma((NY,)), dma((NY, 2)), dma((NY, 2)), dma((NY,)), dma((NY,)),
            dma((29,)), dma((29,)), dma((NZ, NX)), dma((NZ, NX)),
            dma((NZ,)), dma((NZ,)), dma((NY * NX,)), dma((2, NY, NX)), dma((NY * NX,)),
            pltpu.SemaphoreType.REGULAR,
        ],
        compiler_params=pltpu.CompilerParams(
            collective_id=0, has_side_effects=True, vmem_limit_bytes=54912 * 1024
        ),
        name="dedup",
    )(
        embeddings,
        cluster.reshape(1, ROWS),
        order.reshape(1, ROWS),
        query_local.reshape(1, QB),
    )
    return out


def solution(mesh):
    return jax.shard_map(
        body,
        mesh=mesh,
        in_specs=(
            P(("group", "dev"), None),
            P(("group", "dev")),
            P(("group", "dev")),
            P(("group", "dev")),
        ),
        out_specs=P(("group", "dev")),
        check_vma=False,
    )
```
